256 devices in a mesh: col: 16 (over y, x), grp: 16 (over z, core).
Axes of the slice: x: 4, y: 4, z: 8, core: 2. Of those that a mesh axis runs over, the one named last changes fastest.
Arguments:
- table: float32 [256, 131072], P('col', 'grp'), may hold values from -6 to 6
- hot: float32 [256, 8192], P('col'), may hold values from -6 to 6
- accum: float32 [8192], replicated, may hold values from 0.05 to 0.5
- pending: float32 [16, 256, 8192], P('grp', 'col'), may hold values from -0.6 to 0.6
- slot_ids: int32 [2048], replicated, may hold values from 0 to 8191, as said below
- demote_ids: int32 [2048], replicated, may hold values from 0 to 131071, as said below
- promote_ids: int32 [2048], replicated, may hold values from 0 to 131071, as said below
- bag_rows: int32 [4, 8, 32768], P(None, None, 'grp'), may hold values from 0 to 8191
- bag_mask: int32 [4, 8, 32768], P(None, None, 'grp'), may hold values 0 or 1
- labels: int32 [16, 2048], P('col', 'grp'), may hold values 0 or 1
- cross_down: bfloat16 [2048, 512], replicated, may hold values from -0.125 to 0.125
- cross_up: bfloat16 [512, 2048], replicated, may hold values from -0.25 to 0.25
- cross_bias: float32 [2048], replicated, may hold values from -3 to 3
- top_weight: bfloat16 [2048, 1024], replicated, may hold values from -0.125 to 0.125
- top_bias: float32 [1024], replicated, may hold values from -3 to 3
- out_weight: bfloat16 [1024], replicated, may hold values from -0.1875 to 0.1875
Outputs:
- new_table: float32 [256, 131072], P('col', 'grp')
- new_hot: float32 [256, 8192], P('col')
- new_accum: float32 [8192], replicated
- logits: float32 [16, 2048], P('col', 'grp')
The draws below stay inside these ranges and needn't reach their ends.
Inputs may be any that keep to these rules, and one draw needn't show every extreme that they name: `slot_ids`: distinct; includes 0 and 8191. `demote_ids`: distinct; includes 0 and 131071. `promote_ids`: distinct; includes 0 and 131071.
All inputs are finite; a program needn't handle non-finite values. No bound on the sum of `bag_mask` or of `labels` on one device may be relied on, other than what follows from the above.
Results may differ from the reference program's by a relative error of at most 0.006.
Values may be sent and summed in bfloat16 or wider, within the bound.
A program may use at most 192 MiB of HBM per device.

```python
import math
import jax
import jax.numpy as jnp
import numpy as np
from jax import lax

E = 256
F = 8
L = 4
RANK = 512
TOP = 1024
HOT = 8192
Q = 2048
B_DEV = 128
FE = 2048
B_GRP = 2048
SAMPLES = 32768
ROWS = 131072
N_COL = 16
N_GRP = 16


def distinct_ids(key, total, count):
    inner = jax.random.permutation(key, total - 2)[:count - 2] + 1
    ends = jnp.array([0, total - 1], jnp.int32)
    joined = jnp.concatenate([inner.astype(jnp.int32), ends])
    return jax.random.permutation(jax.random.fold_in(key, 1), joined).astype(jnp.int32)


def draw_slot_ids(key, part):
    key = jax.random.fold_in(key, 11)
    return distinct_ids(key, HOT, Q)


def draw_demote_ids(key, part):
    key = jax.random.fold_in(key, 12)
    return distinct_ids(key, ROWS, Q)


def draw_promote_ids(key, part):
    key = jax.random.fold_in(key, 13)
    return distinct_ids(key, ROWS, Q)


def place_ends(values, stream_key, smallest, largest):
    place = [jax.random.randint(jax.random.fold_in(stream_key, axis), (), 0, length) for axis, length in enumerate(values.shape)]
    widest = values.shape.index(max(values.shape))
    next_to = place[:widest] + [(place[widest] + 1) % values.shape[widest]] + place[widest + 1:]
    return values.at[tuple(place)].set(smallest).at[tuple(next_to)].set(largest)


def steps_of(key, dims, cuts, smallest, high):
    factor_of = 1.0
    for dim, blocks in cuts:
        draws = jax.random.uniform(jax.random.fold_in(jax.random.fold_in(key, 6), dim), (blocks,), jnp.float32, smallest / len(cuts), high / len(cuts))
        factor_of = factor_of * jnp.repeat(jnp.exp(draws), dims[dim] // blocks).reshape((-1,) + (1,) * (len(dims) - 1 - dim))
    return factor_of


def cumulative_ranks(count, skew):
    weights = [(1 << 20) // math.isqrt(rank ** skew) + 1 for rank in range(1, count + 1)]
    spread = 1 + sum(weights) // (1 << 30)
    return np.cumsum(np.array([max(1, weight // spread) for weight in weights]))


def skewed_ids(key, dims, amount, skew):
    grid = cumulative_ranks(amount, skew)
    lot = jax.random.randint(jax.random.fold_in(key, 1), dims, 0, int(grid[amount - 1]))
    grade = jnp.searchsorted(jnp.asarray(grid, jnp.int32), lot, side="right")
    return jax.random.permutation(jax.random.fold_in(key, 2), amount)[grade].astype(jnp.int32)


def bell_draw(key, extent, scale, most, cuts=(), held_as=jnp.bfloat16):
    values = scale * jax.random.normal(key, extent, jnp.float32)
    if cuts:
        values = values * steps_of(key, extent, cuts, -0.22, 0.18)
    return jnp.clip(values, -most, most).astype(held_as)


def setup_inputs(seed: int = 0) -> dict:
    arg_keys = jax.random.split(jax.random.key(seed), 17)
    return {
        "table": bell_draw(arg_keys[0], (E, ROWS), 1.0, 6.0, ((0, 16), (1, 16)), jnp.float32),
        "hot": bell_draw(arg_keys[1], (E, HOT), 1.0, 6.0, ((0, 16),), jnp.float32),
        "accum": jnp.clip(jnp.exp(jax.random.uniform(arg_keys[2], (HOT,), jnp.float32, math.log(0.05), math.log(0.5))), 0.05, 0.5),
        "pending": bell_draw(arg_keys[3], (N_GRP, E, HOT), 0.1, 0.6, ((0, 16), (1, 16)), jnp.float32),
        "slot_ids": draw_slot_ids(jax.random.fold_in(arg_keys[16], 71), 0),
        "demote_ids": draw_demote_ids(jax.random.fold_in(arg_keys[16], 71), 0),
        "promote_ids": draw_promote_ids(jax.random.fold_in(arg_keys[16], 71), 0),
        "bag_rows": place_ends(skewed_ids(arg_keys[7], (L, F, SAMPLES), HOT, 2), jax.random.fold_in(arg_keys[7], 3), 0, HOT - 1).astype(jnp.int32),
        "bag_mask": place_ends((jax.random.randint(arg_keys[8], (L, F, SAMPLES), 0, 4) < 3).astype(jnp.int32), jax.random.fold_in(arg_keys[8], 1), 0, 1),
        "labels": place_ends((jax.random.randint(arg_keys[9], (N_COL, N_GRP * B_DEV), 0, 2) < 1).astype(jnp.int32), jax.random.fold_in(arg_keys[9], 1), 0, 1),
        "cross_down": bell_draw(arg_keys[10], (FE, RANK), FE ** -0.5, 0.125),
        "cross_up": bell_draw(arg_keys[11], (RANK, FE), RANK ** -0.5, 0.25),
        "cross_bias": bell_draw(arg_keys[12], (FE,), 0.5, 3.0, (), jnp.float32),
        "top_weight": bell_draw(arg_keys[13], (FE, TOP), FE ** -0.5, 0.125),
        "top_bias": bell_draw(arg_keys[14], (TOP,), 0.5, 3.0, (), jnp.float32),
        "out_weight": bell_draw(arg_keys[15], (TOP,), TOP ** -0.5, 0.1875),
    }


step_size = 0.2
adagrad_eps = 1e-06

def dense_step(x0, label, cross_down, cross_up, cross_bias, top_weight, top_bias, out_weight):
    lowrank = jnp.dot(x0, cross_down, preferred_element_type=jnp.float32).astype(jnp.bfloat16)
    crossgate = jnp.dot(lowrank, cross_up, preferred_element_type=jnp.float32) + cross_bias
    x0_wide = x0.astype(jnp.float32)
    x1 = (x0_wide * crossgate + x0_wide).astype(jnp.bfloat16)
    preact = jnp.dot(x1, top_weight, preferred_element_type=jnp.float32) + top_bias
    sig = jax.nn.sigmoid(preact)
    hidden = (preact * sig).astype(jnp.bfloat16)
    logit = jnp.dot(hidden, out_weight, preferred_element_type=jnp.float32)
    dlogit = jax.nn.sigmoid(logit) - label.astype(jnp.float32)
    slope = sig * (1.0 + preact * (1.0 - sig))
    dhidden = (dlogit[:, None] * out_weight.astype(jnp.float32)[None, :] * slope).astype(jnp.bfloat16)
    dx1 = jnp.dot(dhidden, top_weight.T, preferred_element_type=jnp.float32)
    dgate = (dx1 * x0_wide).astype(jnp.bfloat16)
    dlow = jnp.dot(dgate, cross_up.T, preferred_element_type=jnp.float32).astype(jnp.bfloat16)
    dx0 = (dx1 * (crossgate + 1.0) + jnp.dot(dlow, cross_down.T, preferred_element_type=jnp.float32)).astype(jnp.bfloat16)
    return (logit, dx0)

def reference(table, hot, accum, pending, slot_ids, demote_ids, promote_ids, bag_rows, bag_mask, labels, cross_down, cross_up, cross_bias, top_weight, top_bias, out_weight):
    synced = hot + lax.optimization_barrier(jnp.sum(pending, axis=0))
    new_table = table.at[:, demote_ids].set(synced[:, slot_ids])
    refreshed = synced.at[:, slot_ids].set(new_table[:, promote_ids])
    group_bags = bag_rows.reshape(L, F, N_GRP, B_GRP).transpose(2, 0, 1, 3)
    group_mask = bag_mask.reshape(L, F, N_GRP, B_GRP).transpose(2, 0, 1, 3).astype(jnp.float32)
    group_labels = labels.reshape(N_COL, N_GRP, B_DEV).transpose(1, 0, 2).reshape(N_GRP, B_GRP)

    def one_group(grad, inputs):
        bags, masks, label = inputs
        pooled = jnp.zeros((E, F, B_GRP), jnp.float32)
        for slot in range(L):
            pooled = pooled + refreshed[:, bags[slot]] * masks[slot][None]
        x0 = pooled.astype(jnp.bfloat16).transpose(2, 1, 0).reshape(B_GRP, F * E)
        logit, dx0 = dense_step(x0, label, cross_down, cross_up, cross_bias, top_weight, top_bias, out_weight)
        back = dx0.reshape(B_GRP, F, E).transpose(2, 1, 0).astype(jnp.float32)
        for slot in range(L):
            terms = back * masks[slot][None]
            grad = grad.at[:, bags[slot].reshape(-1)].add(terms.reshape(E, -1))
        return (grad, logit)
    grad, group_logits = lax.scan(one_group, jnp.zeros((E, HOT), jnp.float32), (group_bags, group_mask, group_labels))
    new_accum = accum + lax.optimization_barrier(jnp.mean(grad * grad, axis=0))
    new_hot = refreshed - step_size * grad / jnp.sqrt(new_accum + adagrad_eps)[None, :]
    logits = group_logits.reshape(N_GRP, N_COL, B_DEV).transpose(1, 0, 2).reshape(N_COL, N_GRP * B_DEV)
    return (new_table, new_hot, new_accum, logits)
```

```python
import jax
import jax.numpy as jnp
from jax import lax
from jax.experimental import pallas as pl
from jax.experimental.pallas import tpu as pltpu
from jax.sharding import PartitionSpec as P

E = 256
STEP = 0.2
EPS = 1e-06
MESH = pl.DeviceIdType.MESH
F32 = jnp.float32
BF16 = jnp.bfloat16
I16 = jnp.int16
I32 = jnp.int32
VMEM = pl.BlockSpec(memory_space=pltpu.VMEM)
ANY = pl.BlockSpec(memory_space=pl.ANY)
NT = (((1,), (1,)), ((), ()))
N_SEM = 288
N = 4


def plus(a, d, n):
    return lax.rem(a + d + n, n)


def column(core, a, b):
    return jnp.where(core == 0, b * 4 + a, a * 4 + b)


def pick_lanes(idx, tiles, read):
    idx = jnp.broadcast_to(idx, (8, 128))
    low = idx & 127
    high = idx >> 7
    top = jnp.zeros((8, 128), F32)
    bottom = jnp.zeros((8, 128), F32)
    for t in range(tiles):
        hit = high == t
        a, b = read(t)
        top = jnp.where(hit, jnp.take_along_axis(a, low, axis=1, mode="promise_in_bounds"), top)
        bottom = jnp.where(
            hit, jnp.take_along_axis(b, low, axis=1, mode="promise_in_bounds"), bottom
        )
    return jnp.concatenate([top, bottom], axis=0)


def split(tile):
    tile = tile.astype(F32)
    return tile[0:8], tile[8:16]


def upright(row):
    return jnp.broadcast_to(row, (128, 128)).T


def step_kernel(
    pending, table, hot, accum, slot, demote, promote, label, cross_bias, top_bias, out_weight,
    bag_rows, bag_mask, down_hbm, up_hbm, top_hbm,
    new_table, new_hot, new_accum, logits,
    down, up, top, rows_in, mask_in,
    mine, from_twin, reduced, from_ring, synced, fetched, fetched_in, arrived, match, best, slot_from,
    bags, all_synced, full, fresh, old_in, unit, units, unit_of, wide, bag_col, counts, pooled, for_twin, pooled_in, back, grads,
    evicted, home, fwd_in, side_in, lane_in, far_in, ring_out, ring_in, all_grads, squares, sums,
    load_sem, send_sem, recv_sem,
):
    col = lax.axis_index("col")
    grp = lax.axis_index("grp")
    z, core = lax.div(grp, 2), lax.rem(grp, 2)
    x, y = lax.rem(col, 4), lax.div(col, 4)
    a, b = jnp.where(core == 0, x, y), jnp.where(core == 0, y, x)
    twin = (col, grp + 1 - 2 * core)
    started = []
    used = [0]

    def at(da, db):
        return column(core, plus(a, da, 4), plus(b, db, 4))

    def peer(da, db):
        return (at(da, db), grp)

    def ring(d):
        return (col, plus(z, d, 8) * 2 + core)

    def group(d):
        return (col, plus(grp, d, 16))

    def plane(d):
        return (plus(col, d, 16), grp)

    def go(src, dst, to):
        k = used[0]
        used[0] += 1
        copy = pltpu.make_async_remote_copy(
            src_ref=src, dst_ref=dst, send_sem=send_sem.at[k], recv_sem=recv_sem.at[k],
            device_id=to, device_id_type=MESH,
        )
        copy.start()
        started.append(copy)
        return k

    def landed(k, dst):
        pltpu.make_async_remote_copy(
            src_ref=dst, dst_ref=dst, send_sem=send_sem.at[k], recv_sem=recv_sem.at[k],
            device_id=twin, device_id_type=MESH,
        ).wait_recv()

    loads = [
        pltpu.make_async_copy(src, dst, load_sem.at[i])
        for i, (src, dst) in enumerate(
            (
                (bag_rows.at[:, :, pl.ds(pl.multiple_of(col * 128, 128), 128)], rows_in),
                (bag_mask.at[:, :, pl.ds(pl.multiple_of(col * 128, 128), 128)], mask_in),
                (down_hbm, down),
                (up_hbm, up),
                (top_hbm, top),
            )
        )
    ]
    for load in loads:
        load.start()
    barrier = pltpu.get_barrier_semaphore()
    others = [group(d) for d in range(1, 16)] + [plane(d) for d in range(1, 16)]
    for other in others:
        pl.semaphore_signal(barrier, inc=1, device_id=other, device_id_type=MESH)

    def lanes_of(h, p):
        return pl.ds(pl.multiple_of(h * 4096 + p * 512, 512), 512)

    @pl.loop(0, 16)
    def _(i):
        h, p = lax.div(i, 8), lax.rem(i, 8)
        mine[h, p] = pending[:, lanes_of(h, p)]

    best[...] = jnp.full_like(best, -1)

    @pl.loop(0, 16)
    def _(t):
        dem, slo = upright(demote[pl.ds(t, 1), :]), upright(slot[pl.ds(t, 1), :])
        for j in range(16):
            hit = jnp.where(dem == promote[j : j + 1, :], slo, -1)
            best[j] = jnp.maximum(best[j], jnp.max(hit.reshape(16, 8, 128), axis=0))

    for j in range(16):
        match[j : j + 1, :] = jnp.max(best[j], axis=0, keepdims=True)

    @pl.loop(0, 16)
    def _(t):
        idx = promote[pl.ds(t, 1), :] - grp * 8192
        idx = jnp.where((match[pl.ds(t, 1), :] < 0) & (idx >= 0) & (idx < 8192), idx, -1)
        fetched[t] = pick_lanes(
            idx, 64, lambda s: split(table[:, s * 128 : (s + 1) * 128])
        )

    loads[0].wait()
    loads[1].wait()
    bags[0] = jnp.where(mask_in[...] > 0, rows_in[...], -1)
    pl.semaphore_wait(barrier, len(others))

    k_twin = go(mine.at[1 - core], from_twin, twin)

    k_bags = go(bags.at[0], bags.at[1], twin)

    def stand(which):
        @pl.loop(0, 32)
        def _(i):
            l, f = lax.div(i, 8), lax.rem(i, 8)
            row = upright(bags[which, l, pl.ds(f, 1), :] - core * 4096)
            bag_col[l, pl.ds(pl.multiple_of(which * 1024 + f * 128, 128), 128), :] = row.astype(I16)

    stand(0)
    landed(k_twin, from_twin)
    reduced[...] = mine[core] + from_twin[...]
    k_ring = [go(reduced.at[plus(z, d, 8)], from_ring.at[d], ring(d)) for d in range(1, 8)]

    def count(lo, hi):
        @pl.loop(lo, hi)
        def _(i):
            r = pl.ds(pl.multiple_of(i * 16, 16), 16)
            lane = lax.broadcasted_iota(I32, (16, 128), 1)
            idx = [bag_col[l, r, :].astype(I32) for l in range(4)]
            low = [jnp.where((v & 127) == lane, 1.0, 0.0).astype(BF16) for v in idx]
            high = [(v >> 7).astype(F32).astype(BF16) for v in idx]
            zero = jnp.zeros((16, 128), BF16)
            for t in range(32):
                acc = None
                for l in range(4):
                    hit = jnp.where(high[l] == BF16(t), low[l], zero)
                    acc = hit if acc is None else acc + hit
                counts[r, t * 128 : (t + 1) * 128] = acc

    def origin(ids, first, places, half_rows):
        ids = ids - first
        lane = ids & 127
        high = ids >> 7
        j = lax.broadcasted_iota(I32, (1, 2048), 1)
        sub = lax.broadcasted_iota(I32, (128, 2048), 0)
        here = sub == lane
        major = jnp.where(here, (j >> 7).astype(F32), 0.0).astype(BF16)
        minor = jnp.where(here, (j & 127).astype(F32) + 1.0, 0.0).astype(BF16)
        rows = lax.broadcasted_iota(I32, (half_rows, 2048), 0)
        pick = jnp.where(rows == high, 1.0, 0.0).astype(BF16)
        major = lax.dot_general(pick, major, NT, preferred_element_type=F32)
        minor = lax.dot_general(pick, minor, NT, preferred_element_type=F32)
        return (major * 128.0 + minor).astype(I32) - 1

    def flat(ref):
        return jnp.concatenate([ref[t : t + 1, :] for t in range(16)], axis=1)

    slot_from[...] = origin(flat(slot), core * 4096, 4096, 32)
    home[...] = origin(flat(demote), grp * 8192, 8192, 64)
    count(0, 40)
    total = reduced[z]
    for d in range(1, 8):
        landed(k_ring[d - 1], from_ring.at[d])
        total = total + from_ring[d]
    base = core * 4096 + z * 512
    synced[...] = total + hot[:, pl.ds(pl.multiple_of(base, 512), 512)]

    @pl.loop(0, 16)
    def _(t):
        again = match[pl.ds(t, 1), :] - base
        value = pick_lanes(again, 4, lambda s: split(synced[:, s * 128 : (s + 1) * 128]))
        fetched[t] = value + fetched[t]

    k_fet = [go(fetched.at[plus(grp, d, 16)], fetched_in.at[d], group(d)) for d in range(1, 16)]
    all_synced[grp] = synced[...]
    k_syn = [go(all_synced.at[grp], all_synced.at[grp], ring(d)) for d in range(1, 8)]
    k_hand = [go(all_synced.at[grp], all_synced.at[grp], twin)]
    landed(k_bags, bags.at[1])
    stand(1)
    count(40, 84)
    mine_now = fetched[grp]
    for d in range(1, 16):
        landed(k_fet[d - 1], fetched_in.at[d])
        mine_now = mine_now + fetched_in[d]
    arrived[grp] = mine_now
    k_arr = [go(arrived.at[grp], arrived.at[grp], group(d)) for d in range(1, 16)]
    count(84, 128)
    for d in range(1, 8):
        there = all_synced.at[plus(z, -d, 8) * 2 + core]
        landed(k_syn[d - 1], there)
        k_hand.append(go(there, there, twin))
    for d in range(1, 16):
        landed(k_arr[d - 1], arrived.at[plus(grp, -d, 16)])

    def renew(lo, hi):
        @pl.loop(lo, hi)
        def _(p):
            for i in range(4):
                idx = slot_from[pl.ds(p * 4 + i, 1), :]
                lanes = slice(i * 128, (i + 1) * 128)
                picked = pick_lanes(idx, 16, lambda s: split(arrived[s]))
                old = all_synced[p * 2 + core, :, lanes]
                value = jnp.where(jnp.broadcast_to(idx, (16, 128)) >= 0, picked, old)
                fresh[p, :, lanes] = value
                unit[pl.ds(p * 4 + i, 1), :] = jnp.max(jnp.abs(value), axis=0, keepdims=True)

    def encode():
        units[col] = (jnp.maximum(unit[...], 1e-30) * (1.008 / 32000.0)).astype(BF16)
        unit[...] = 1.0 / units[col].astype(F32)

        @pl.loop(0, 8)
        def _(p):
            for i in range(4):
                lanes = slice(i * 128, (i + 1) * 128)
                code = jnp.round(fresh[p, :, lanes] * unit[pl.ds(p * 4 + i, 1), :])
                full[col, p, :, lanes] = code.astype(I32).astype(I16)

    def decode(c):
        unit_of[...] = units[c].astype(F32)

        @pl.loop(0, 8)
        def _(p):
            for i in range(4):
                lanes = slice(i * 128, (i + 1) * 128)
                value = full[c, p, :, lanes].astype(I32).astype(F32)
                value = value * unit_of[pl.ds(p * 4 + i, 1), :]
                high = value.astype(BF16)
                wide[0, p, c, :, lanes] = high
                wide[1, p, c, :, lanes] = (value - high.astype(F32)).astype(BF16)

    def demoted(lo, hi):
        @pl.loop(lo, hi)
        def _(t):
            evicted[t] = pick_lanes(
                slot[pl.ds(t, 1), :], 64,
                lambda s: split(
                    all_synced[
                        (s % 32 // 4) * 2 + s // 32, :, (s % 4) * 128 : (s % 4 + 1) * 128
                    ]
                ),
            )

    def table_out(lo, hi):
        @pl.loop(lo, hi)
        def _(q):
            for u in range(4):
                lanes = pl.ds(pl.multiple_of(q * 512 + u * 128, 128), 128)
                idx = home[pl.ds(q * 4 + u, 1), :]
                picked = pick_lanes(idx, 16, lambda s: (evicted[s, 0:8, :], evicted[s, 8:16, :]))
                new_table[:, lanes] = jnp.where(
                    jnp.broadcast_to(idx, (16, 128)) >= 0, picked, table[:, lanes]
                )

    def widen():
        half = pl.ds(0, 4), pl.ds(4, 4)

        def block(da, db, which=None):
            ref = full.at[at(da, db)]
            return ref if which is None else ref.at[half[which]]

        def pass_on(ref, to):
            return go(ref, ref, to)

        def along_b(da):
            return pass_on(block(da, 0), peer(0, 1)), pass_on(block(da, 0), peer(0, -1))

        right = pass_on(block(0, 0), peer(1, 0))
        left = pass_on(block(0, 0), peer(-1, 0))
        pairs = {0: along_b(0)}
        more = {}

        def along_b_more(da):
            landed(pairs[da][0], block(da, -1))
            first = pass_on(block(da, -1, 0), peer(0, 1))
            landed(pairs[da][1], block(da, 1))
            more[da] = first, pass_on(block(da, 1, 1), peer(0, -1))
            decode(at(da, -1))
            decode(at(da, 1))

        yield
        decode(col)
        landed(right, block(-1, 0))
        on_right = pass_on(block(-1, 0, 0), peer(1, 0))
        pairs[-1] = along_b(-1)
        yield
        landed(left, block(1, 0))
        on_left = pass_on(block(1, 0, 1), peer(-1, 0))
        pairs[1] = along_b(1)
        yield
        along_b_more(0)
        yield
        landed(on_right, block(2, 0, 0))
        landed(on_left, block(2, 0, 1))
        pairs[2] = along_b(2)
        for da in (-1, 1, 2):
            decode(at(da, 0))
        for da in (-1, 1, 2):
            yield
            along_b_more(da)
        for da in (0, -1, 1, 2):
            yield
            landed(more[da][0], block(da, 2, 0))
            landed(more[da][1], block(da, 2, 1))
            decode(at(da, 2))

    def look(first, out):
        acc = None
        for p in range(8):
            some = counts[pl.ds(pl.multiple_of(first, 256), 256), p * 512 : (p + 1) * 512]
            for k in range(2):
                term = lax.dot_general(
                    some, wide[k, p].reshape(256, 512), NT, preferred_element_type=F32
                )
                acc = term if acc is None else acc + term
        out[...] = acc

    renew(0, 8)
    encode()
    travel = widen()
    next(travel)
    k_unit = [go(units.at[col], units.at[col], plane(d)) for d in range(1, 16)]
    k_old = go(fresh, old_in, twin)
    for d in range(8):
        landed(k_hand[d], all_synced.at[plus(z, -d, 8) * 2 + 1 - core])
    next(travel)
    next(travel)
    for d in range(1, 16):
        landed(k_unit[d - 1], units.at[plus(col, -d, 16)])
    for _ in travel:
        pass

    k_pool = []
    for m in range(4):
        look(1024 + m * 256, for_twin.at[m])
        k_pool.append(go(for_twin.at[m], pooled_in.at[m], twin))

    @pl.loop(0, 4)
    def _(m):
        look(m * 256, pooled.at[m])

    for m in range(4):
        landed(k_pool[m], pooled_in.at[m])

    for load in loads[2:]:
        load.wait()
    both = [(pooled[m] + pooled_in[m]).astype(BF16) for m in range(4)]
    x0 = jnp.concatenate(
        [both[f // 2][f % 2 * 128 : f % 2 * 128 + 128] for f in range(8)], axis=1
    )
    low = jnp.dot(x0, down[...], preferred_element_type=F32).astype(BF16)
    gate = jnp.dot(low, up[...], preferred_element_type=F32) + cross_bias[...]
    wide0 = x0.astype(F32)
    x1 = (wide0 * gate + wide0).astype(BF16)
    pre = jnp.dot(x1, top[...], preferred_element_type=F32) + top_bias[...]
    sig = jax.nn.sigmoid(pre)
    hidden = (pre * sig).astype(BF16).astype(F32)
    weight = out_weight[...].astype(F32).reshape(1, 1024)
    logit = jnp.sum(hidden * weight, axis=1, keepdims=True)
    across = jnp.broadcast_to(logit, (128, 128)).T
    logits[...] = across[0:1, :]
    dlogit = jax.nn.sigmoid(across) - label[...].astype(F32)
    dlogit = dlogit.T[:, 0:1]
    slope = sig * (1.0 + pre * (1.0 - sig))
    dhidden = (dlogit * weight * slope).astype(BF16)
    dx1 = lax.dot_general(dhidden, top[...], NT, preferred_element_type=F32)
    dgate = (dx1 * wide0).astype(BF16)
    dlow = lax.dot_general(dgate, up[...], NT, preferred_element_type=F32).astype(BF16)
    k_back = []
    for c in range(4):
        lanes = slice(c * 512, (c + 1) * 512)
        dx0 = dx1[:, lanes] * (gate[:, lanes] + 1.0) + lax.dot_general(
            dlow, down[lanes, :], NT, preferred_element_type=F32
        )
        for f in range(2):
            back[c, :, f * 128 : (f + 1) * 128] = dx0[:, f * 256 : (f + 1) * 256].T.astype(BF16)
        k_back.append(go(back.at[c], back.at[4 + c], twin))

    for c in range(4):
        landed(k_back[c], back.at[4 + c])

    def slopes(lo, hi):
        @pl.loop(lo, hi)
        def _(p):
            lanes = pl.ds(pl.multiple_of(p * 512, 512), 512)
            acc = None
            for c in range(8):
                term = jnp.dot(
                    back[c], counts[c * 256 : (c + 1) * 256, lanes], preferred_element_type=F32
                )
                acc = term if acc is None else acc + term
            grads[:, p] = acc.astype(BF16).reshape(16, 16, 512)

    def add(ref, other):
        ref[...] = (ref[...].astype(F32) + other[...].astype(F32)).astype(BF16)

    order = [(da, db) for da in (2, 1, -1, 0) for db in (2, 1, -1, 0)]

    def narrow(s):
        whole = pl.ds(s * N, N)
        lo, hi = pl.ds(s * N, N // 2), pl.ds(s * N + N // 2, N // 2)
        few = pl.ds(s * N // 2, N // 2)
        ways = [{} for _ in range(4)]
        last = {}

        def first_part(i):
            for j in range(4):
                k = i * 4 + j
                where = at(*order[k])
                if j == 0:
                    ways[i][0] = go(grads.at[where, lo], fwd_in.at[i, 0, few], peer(0, 1))
                    ways[i][1] = go(grads.at[where, hi], fwd_in.at[i, 1, few], peer(0, -1))
                if j == 1:
                    ways[i][2] = go(grads.at[where, hi], side_in.at[i, 0, hi], peer(0, 1))
                if j == 2:
                    ways[i][3] = go(grads.at[where, lo], side_in.at[i, 1, lo], peer(0, -1))

        def second_part(i):
            landed(ways[i][0], fwd_in.at[i, 0, few])
            add(grads.at[at(*order[i * 4 + 1]), lo], fwd_in.at[i, 0, few])
            ways[i][4] = go(grads.at[at(*order[i * 4 + 1]), lo], side_in.at[i, 0, lo], peer(0, 1))
            landed(ways[i][1], fwd_in.at[i, 1, few])
            add(grads.at[at(*order[i * 4 + 2]), hi], fwd_in.at[i, 1, few])
            ways[i][5] = go(grads.at[at(*order[i * 4 + 2]), hi], side_in.at[i, 1, hi], peer(0, -1))

        def third_part(i):
            landed(ways[i][2], side_in.at[i, 0, hi])
            landed(ways[i][3], side_in.at[i, 1, lo])
            landed(ways[i][4], side_in.at[i, 0, lo])
            landed(ways[i][5], side_in.at[i, 1, hi])
            where = at(*order[i * 4 + 3])
            grads[where, whole] = (
                grads[where, whole].astype(F32)
                + side_in[i, 0, whole].astype(F32)
                + side_in[i, 1, whole].astype(F32)
            ).astype(BF16)

        def last_axis(i):
            where = at(*order[i * 4 + 3])
            if i == 0:
                last[0] = go(grads.at[where, lo], far_in.at[0, few], peer(1, 0))
                last[1] = go(grads.at[where, hi], far_in.at[1, few], peer(-1, 0))
            if i == 1:
                last[2] = go(grads.at[where, hi], lane_in.at[0, hi], peer(1, 0))
                landed(last[0], far_in.at[0, few])
                add(grads.at[where, lo], far_in.at[0, few])
                last[4] = go(grads.at[where, lo], lane_in.at[0, lo], peer(1, 0))
            if i == 2:
                last[3] = go(grads.at[where, lo], lane_in.at[1, lo], peer(-1, 0))
                landed(last[1], far_in.at[1, few])
                add(grads.at[where, hi], far_in.at[1, few])
                last[5] = go(grads.at[where, hi], lane_in.at[1, hi], peer(-1, 0))

        def begin():
            for i in range(4):
                first_part(i)

        def more(*parts):
            for i in parts:
                second_part(i)

        def turn(i):
            third_part(i)
            last_axis(i)

        def finish():
            turn(3)
            landed(last[2], lane_in.at[0, hi])
            landed(last[3], lane_in.at[1, lo])
            landed(last[4], lane_in.at[0, lo])
            landed(last[5], lane_in.at[1, hi])
            ring_out[whole] = (
                grads[col, whole].astype(F32)
                + lane_in[0, whole].astype(F32)
                + lane_in[1, whole].astype(F32)
            ).astype(BF16)

        return begin, more, turn, finish

    slopes(0, 4)
    begin0, more0, turn0, finish0 = narrow(0)
    begin1, more1, turn1, finish1 = narrow(1)
    begin0()
    slopes(4, 6)
    more0(0, 1)
    slopes(6, 8)
    begin1()
    more0(2, 3)
    turn0(0)
    turn0(1)
    more1(0, 1)
    turn0(2)
    more1(2, 3)
    turn1(0)
    turn1(1)
    finish0()
    turn1(2)
    finish1()

    k_ring = [go(ring_out.at[plus(z, d, 8)], ring_in.at[d], ring(d)) for d in range(1, 8)]
    demoted(0, 16)
    grad = ring_out[z].astype(F32)
    for d in range(1, 8):
        landed(k_ring[d - 1], ring_in.at[d])
        grad = grad + ring_in[d].astype(F32)
    square = jnp.sum(grad * grad, axis=0, keepdims=True)
    square = [square[:, i * 128 : (i + 1) * 128] for i in range(4)]
    squares[col] = jnp.concatenate(square + square, axis=0)
    k_sq = [go(squares.at[col], squares.at[col], plane(d)) for d in range(1, 16)]
    all_grads[grp] = grad.astype(BF16)
    k_all = [go(all_grads.at[grp], all_grads.at[grp], ring(d)) for d in range(1, 8)]
    k_hand = [go(all_grads.at[grp], all_grads.at[grp], twin)]
    table_out(0, 9)
    for d in range(1, 16):
        landed(k_sq[d - 1], squares.at[plus(col, -d, 16)])
    before = accum[pl.ds(core * 32 + z * 4, 4), :]
    sums[grp] = jnp.concatenate([before, before], axis=0) + jnp.sum(squares[...], axis=0) / E
    k_sum = [go(sums.at[grp], sums.at[grp], group(d)) for d in range(1, 16)]
    table_out(9, 16)
    for d in range(1, 8):
        there = all_grads.at[plus(z, -d, 8) * 2 + core]
        landed(k_all[d - 1], there)
        k_hand.append(go(there, there, twin))
    for d in range(8):
        landed(k_hand[d], all_grads.at[plus(z, -d, 8) * 2 + 1 - core])
    for d in range(1, 16):
        landed(k_sum[d - 1], sums.at[plus(grp, -d, 16)])
    landed(k_old, old_in)
    for h in range(2):
        for p in range(8):
            new_accum[h * 32 + p * 4 : h * 32 + p * 4 + 4, :] = sums[p * 2 + h, 0:4, :]

        @pl.loop(0, 8)
        def _(p):
            g = p * 2 + h
            for i in range(4):
                lanes = pl.ds(pl.multiple_of(h * 4096 + p * 512 + i * 128, 128), 128)
                inner = slice(i * 128, (i + 1) * 128)
                scale = STEP / jnp.sqrt(sums[g, i : i + 1, :] + EPS)
                old = jnp.where(core == h, fresh[p, :, inner], old_in[p, :, inner])
                new_hot[:, lanes] = old - all_grads[g, :, inner].astype(F32) * scale

    for copy in started:
        copy.wait_send()


def step(*args):
    dma = pltpu.SemaphoreType.DMA
    v = pltpu.VMEM
    return pl.pallas_call(
        step_kernel,
        out_shape=[
            jax.ShapeDtypeStruct((16, 8192), F32),
            jax.ShapeDtypeStruct((16, 8192), F32),
            jax.ShapeDtypeStruct((64, 128), F32),
            jax.ShapeDtypeStruct((1, 128), F32),
        ],
        in_specs=[VMEM] * 11 + [ANY] * 5,
        out_specs=[VMEM] * 4,
        scratch_shapes=[
            v((2048, 512), BF16),
            v((512, 2048), BF16),
            v((2048, 1024), BF16),
            v((4, 8, 128), I32),
            v((4, 8, 128), I32),
            v((2, 8, 16, 512), F32),
            v((8, 16, 512), F32),
            v((8, 16, 512), F32),
            v((8, 16, 512), F32),
            v((16, 512), F32),
            v((16, 16, 128), F32),
            v((16, 16, 128), F32),
            v((16, 16, 128), F32),
            v((16, 128), I32),
            v((16, 8, 128), I32),
            v((32, 128), I32),
            v((2, 4, 8, 128), I32),
            v((16, 16, 512), F32),
            v((16, 8, 16, 512), I16),
            v((8, 16, 512), F32),
            v((8, 16, 512), F32),
            v((32, 128), F32),
            v((16, 32, 128), BF16),
            v((32, 128), F32),
            v((2, 8, 16, 16, 512), BF16),
            v((4, 2048, 128), I16),
            v((2048, 4096), BF16),
            v((4, 256, 256), F32),
            v((4, 256, 256), F32),
            v((4, 256, 256), F32),
            v((8, 256, 256), BF16),
            v((16, 8, 16, 512), BF16),
            v((16, 16, 128), F32),
            v((64, 128), I32),
            v((4, 2, 4, 16, 512), BF16),
            v((4, 2, 8, 16, 512), BF16),
            v((2, 8, 16, 512), BF16),
            v((2, 4, 16, 512), BF16),
            v((8, 16, 512), BF16),
            v((8, 16, 512), BF16),
            v((16, 16, 512), BF16),
            v((16, 8, 128), F32),
            v((16, 8, 128), F32),
            dma((5,)),
            dma((N_SEM,)),
            dma((N_SEM,)),
        ],
        compiler_params=pltpu.CompilerParams(
            collective_id=0, has_side_effects=True, vmem_limit_bytes=62 << 20
        ),
    )(*args)


def hand_out_kernel(*refs):
    n = len(refs) // 2
    for i in range(n):
        refs[n + i][...] = refs[i][...]


def hand_out(*arrays):
    return pl.pallas_call(
        hand_out_kernel,
        out_shape=[jax.ShapeDtypeStruct(a.shape, a.dtype) for a in arrays],
        in_specs=[VMEM] * len(arrays),
        out_specs=[VMEM] * len(arrays),
    )(*arrays)


def per_device(
    table, hot, accum, pending, slot_ids, demote_ids, promote_ids, bag_rows, bag_mask, labels,
    cross_down, cross_up, cross_bias, top_weight, top_bias, out_weight,
):
    outputs = step(
        pending[0], table, hot, accum.reshape(64, 128), slot_ids.reshape(16, 128),
        demote_ids.reshape(16, 128), promote_ids.reshape(16, 128), labels, cross_bias[None],
        top_bias[None], out_weight, bag_rows, bag_mask, cross_down, cross_up, top_weight,
    )
    new_table, new_hot, new_accum, logits = hand_out(*outputs)
    return new_table, new_hot, new_accum.reshape(8192), logits


def solution(mesh):
    return jax.shard_map(
        per_device,
        mesh=mesh,
        in_specs=(
            P("col", "grp"), P("col", None), P(), P("grp", "col", None), P(), P(), P(),
            P(None, None, "grp"), P(None, None, "grp"), P("col", "grp"),
            P(), P(), P(), P(), P(), P(),
        ),
        out_specs=(P("col", "grp"), P("col", None), P(), P("col", "grp")),
        check_vma=False,
    )
```

```python
import jax
import jax.numpy as jnp
from jax import lax
from jax.experimental import pallas as pl
from jax.experimental.pallas import tpu as pltpu
from jax.sharding import PartitionSpec as P

E = 256
STEP = 0.2
EPS = 1e-06
MESH = pl.DeviceIdType.MESH
F32 = jnp.float32
BF16 = jnp.bfloat16
I16 = jnp.int16
I32 = jnp.int32
VMEM = pl.BlockSpec(memory_space=pltpu.VMEM)
ANY = pl.BlockSpec(memory_space=pl.ANY)
NT = (((1,), (1,)), ((), ()))
N_SEM = 288
N = 4


def plus(a, d, n):
    return lax.rem(a + d + n, n)


def column(core, a, b):
    return jnp.where(core == 0, b * 4 + a, a * 4 + b)


def pick_lanes(idx, tiles, read):
    idx = jnp.broadcast_to(idx, (8, 128))
    low = idx & 127
    high = idx >> 7
    top = jnp.zeros((8, 128), F32)
    bottom = jnp.zeros((8, 128), F32)
    for t in range(tiles):
        hit = high == t
        a, b = read(t)
        top = jnp.where(hit, jnp.take_along_axis(a, low, axis=1, mode="promise_in_bounds"), top)
        bottom = jnp.where(
            hit, jnp.take_along_axis(b, low, axis=1, mode="promise_in_bounds"), bottom
        )
    return jnp.concatenate([top, bottom], axis=0)


def split(tile):
    tile = tile.astype(F32)
    return tile[0:8], tile[8:16]


def upright(row):
    return jnp.broadcast_to(row, (128, 128)).T


def step_kernel(
    pending, table, hot, accum, slot, demote, promote, label, cross_bias, top_bias, out_weight,
    bag_rows, bag_mask, down_hbm, up_hbm, top_hbm,
    new_table, new_hot, new_accum, logits,
    down, up, top, rows_in, mask_in,
    mine, from_twin, reduced, from_ring, synced, fetched, fetched_in, arrived, match, best, slot_from,
    bags, all_synced, full, fresh, old_in, unit, units, unit_of, wide, bag_col, counts, pooled, for_twin, pooled_in, back, grads,
    evicted, home, fwd_in, side_in, lane_in, far_in, ring_out, ring_in, all_grads, squares, sums,
    load_sem, send_sem, recv_sem,
):
    col = lax.axis_index("col")
    grp = lax.axis_index("grp")
    z, core = lax.div(grp, 2), lax.rem(grp, 2)
    x, y = lax.rem(col, 4), lax.div(col, 4)
    a, b = jnp.where(core == 0, x, y), jnp.where(core == 0, y, x)
    twin = (col, grp + 1 - 2 * core)
    started = []
    used = [0]

    def at(da, db):
        return column(core, plus(a, da, 4), plus(b, db, 4))

    def peer(da, db):
        return (at(da, db), grp)

    def ring(d):
        return (col, plus(z, d, 8) * 2 + core)

    def group(d):
        return (col, plus(grp, d, 16))

    def plane(d):
        return (plus(col, d, 16), grp)

    def go(src, dst, to):
        k = used[0]
        used[0] += 1
        copy = pltpu.make_async_remote_copy(
            src_ref=src, dst_ref=dst, send_sem=send_sem.at[k], recv_sem=recv_sem.at[k],
            device_id=to, device_id_type=MESH,
        )
        copy.start()
        started.append(copy)
        return k

    def landed(k, dst):
        pltpu.make_async_remote_copy(
            src_ref=dst, dst_ref=dst, send_sem=send_sem.at[k], recv_sem=recv_sem.at[k],
            device_id=twin, device_id_type=MESH,
        ).wait_recv()

    loads = [
        pltpu.make_async_copy(src, dst, load_sem.at[i])
        for i, (src, dst) in enumerate(
            (
                (bag_rows.at[:, :, pl.ds(pl.multiple_of(col * 128, 128), 128)], rows_in),
                (bag_mask.at[:, :, pl.ds(pl.multiple_of(col * 128, 128), 128)], mask_in),
                (down_hbm, down),
                (up_hbm, up),
                (top_hbm, top),
            )
        )
    ]
    for load in loads:
        load.start()
    barrier = pltpu.get_barrier_semaphore()
    others = [group(d) for d in range(1, 16)] + [plane(d) for d in range(1, 16)]
    for other in others:
        pl.semaphore_signal(barrier, inc=1, device_id=other, device_id_type=MESH)

    def lanes_of(h, p):
        return pl.ds(pl.multiple_of(h * 4096 + p * 512, 512), 512)

    @pl.loop(0, 16)
    def _(i):
        h, p = lax.div(i, 8), lax.rem(i, 8)
        mine[h, p] = pending[:, lanes_of(h, p)]

    best[...] = jnp.full_like(best, -1)

    @pl.loop(0, 16)
    def _(t):
        dem, slo = upright(demote[pl.ds(t, 1), :]), upright(slot[pl.ds(t, 1), :])
        for j in range(16):
            hit = jnp.where(dem == promote[j : j + 1, :], slo, -1)
            best[j] = jnp.maximum(best[j], jnp.max(hit.reshape(16, 8, 128), axis=0))

    for j in range(16):
        match[j : j + 1, :] = jnp.max(best[j], axis=0, keepdims=True)

    @pl.loop(0, 16)
    def _(t):
        idx = promote[pl.ds(t, 1), :] - grp * 8192
        idx = jnp.where((match[pl.ds(t, 1), :] < 0) & (idx >= 0) & (idx < 8192), idx, -1)
        fetched[t] = pick_lanes(
            idx, 64, lambda s: split(table[:, s * 128 : (s + 1) * 128])
        )

    loads[0].wait()
    loads[1].wait()
    bags[0] = jnp.where(mask_in[...] > 0, rows_in[...], -1)
    pl.semaphore_wait(barrier, len(others))

    k_twin = go(mine.at[1 - core], from_twin, twin)

    k_bags = go(bags.at[0], bags.at[1], twin)

    def stand(which):
        @pl.loop(0, 32)
        def _(i):
            l, f = lax.div(i, 8), lax.rem(i, 8)
            row = upright(bags[which, l, pl.ds(f, 1), :] - core * 4096)
            bag_col[l, pl.ds(pl.multiple_of(which * 1024 + f * 128, 128), 128), :] = row.astype(I16)

    stand(0)
    landed(k_twin, from_twin)
    reduced[...] = mine[core] + from_twin[...]
    k_ring = [go(reduced.at[plus(z, d, 8)], from_ring.at[d], ring(d)) for d in range(1, 8)]

    def count(lo, hi):
        @pl.loop(lo, hi)
        def _(i):
            r = pl.ds(pl.multiple_of(i * 16, 16), 16)
            lane = lax.broadcasted_iota(I32, (16, 128), 1)
            idx = [bag_col[l, r, :].astype(I32) for l in range(4)]
            low = [jnp.where((v & 127) == lane, 1.0, 0.0).astype(BF16) for v in idx]
            high = [(v >> 7).astype(F32).astype(BF16) for v in idx]
            zero = jnp.zeros((16, 128), BF16)
            for t in range(32):
                acc = None
                for l in range(4):
                    hit = jnp.where(high[l] == BF16(t), low[l], zero)
                    acc = hit if acc is None else acc + hit
                counts[r, t * 128 : (t + 1) * 128] = acc

    def origin(ids, first, places, half_rows):
        ids = ids - first
        lane = ids & 127
        high = ids >> 7
        j = lax.broadcasted_iota(I32, (1, 2048), 1)
        sub = lax.broadcasted_iota(I32, (128, 2048), 0)
        here = sub == lane
        major = jnp.where(here, (j >> 7).astype(F32), 0.0).astype(BF16)
        minor = jnp.where(here, (j & 127).astype(F32) + 1.0, 0.0).astype(BF16)
        rows = lax.broadcasted_iota(I32, (half_rows, 2048), 0)
        pick = jnp.where(rows == high, 1.0, 0.0).astype(BF16)
        major = lax.dot_general(pick, major, NT, preferred_element_type=F32)
        minor = lax.dot_general(pick, minor, NT, preferred_element_type=F32)
        return (major * 128.0 + minor).astype(I32) - 1

    def flat(ref):
        return jnp.concatenate([ref[t : t + 1, :] for t in range(16)], axis=1)

    slot_from[...] = origin(flat(slot), core * 4096, 4096, 32)
    home[...] = origin(flat(demote), grp * 8192, 8192, 64)
    count(0, 40)
    total = reduced[z]
    for d in range(1, 8):
        landed(k_ring[d - 1], from_ring.at[d])
        total = total + from_ring[d]
    base = core * 4096 + z * 512
    synced[...] = total + hot[:, pl.ds(pl.multiple_of(base, 512), 512)]

    @pl.loop(0, 16)
    def _(t):
        again = match[pl.ds(t, 1), :] - base
        value = pick_lanes(again, 4, lambda s: split(synced[:, s * 128 : (s + 1) * 128]))
        fetched[t] = value + fetched[t]

    k_fet = [go(fetched.at[plus(grp, d, 16)], fetched_in.at[d], group(d)) for d in range(1, 16)]
    all_synced[grp] = synced[...]
    k_syn = [go(all_synced.at[grp], all_synced.at[grp], ring(d)) for d in range(1, 8)]
    k_hand = [go(all_synced.at[grp], all_synced.at[grp], twin)]
    landed(k_bags, bags.at[1])
    stand(1)
    count(40, 84)
    mine_now = fetched[grp]
    for d in range(1, 16):
        landed(k_fet[d - 1], fetched_in.at[d])
        mine_now = mine_now + fetched_in[d]
    arrived[grp] = mine_now
    k_arr = [go(arrived.at[grp], arrived.at[grp], group(d)) for d in range(1, 16)]
    count(84, 128)
    for d in range(1, 8):
        there = all_synced.at[plus(z, -d, 8) * 2 + core]
        landed(k_syn[d - 1], there)
        k_hand.append(go(there, there, twin))
    for d in range(1, 16):
        landed(k_arr[d - 1], arrived.at[plus(grp, -d, 16)])

    def renew(lo, hi):
        @pl.loop(lo, hi)
        def _(p):
            for i in range(4):
                idx = slot_from[pl.ds(p * 4 + i, 1), :]
                lanes = slice(i * 128, (i + 1) * 128)
                picked = pick_lanes(idx, 16, lambda s: split(arrived[s]))
                old = all_synced[p * 2 + core, :, lanes]
                value = jnp.where(jnp.broadcast_to(idx, (16, 128)) >= 0, picked, old)
                fresh[p, :, lanes] = value
                unit[pl.ds(p * 4 + i, 1), :] = jnp.max(jnp.abs(value), axis=0, keepdims=True)

    def encode(s):
        @pl.loop(s * N, s * N + N)
        def _(p):
            for i in range(4):
                lanes = slice(i * 128, (i + 1) * 128)
                code = jnp.round(fresh[p, :, lanes] * unit[pl.ds(p * 4 + i, 1), :])
                full[col, p, :, lanes] = code.astype(I32).astype(I16)

    def decode(c, s):
        unit_of[...] = units[c].astype(F32)

        @pl.loop(s * N, s * N + N)
        def _(p):
            for i in range(4):
                lanes = slice(i * 128, (i + 1) * 128)
                value = full[c, p, :, lanes].astype(I32).astype(F32)
                value = value * unit_of[pl.ds(p * 4 + i, 1), :]
                high = value.astype(BF16)
                wide[0, p, c, :, lanes] = high
                wide[1, p, c, :, lanes] = (value - high.astype(F32)).astype(BF16)

    def demoted(lo, hi):
        @pl.loop(lo, hi)
        def _(t):
            evicted[t] = pick_lanes(
                slot[pl.ds(t, 1), :], 64,
                lambda s: split(
                    all_synced[
                        (s % 32 // 4) * 2 + s // 32, :, (s % 4) * 128 : (s % 4 + 1) * 128
                    ]
                ),
            )

    def table_out(lo, hi):
        @pl.loop(lo, hi)
        def _(q):
            for u in range(4):
                lanes = pl.ds(pl.multiple_of(q * 512 + u * 128, 128), 128)
                idx = home[pl.ds(q * 4 + u, 1), :]
                picked = pick_lanes(idx, 16, lambda s: (evicted[s, 0:8, :], evicted[s, 8:16, :]))
                new_table[:, lanes] = jnp.where(
                    jnp.broadcast_to(idx, (16, 128)) >= 0, picked, table[:, lanes]
                )

    def widen(s):
        whole = pl.ds(s * N, N)
        half = pl.ds(s * N, N // 2), pl.ds(s * N + N // 2, N // 2)

        def block(da, db, which=None):
            return full.at[at(da, db), whole if which is None else half[which]]

        def pass_on(ref, to):
            return go(ref, ref, to)

        def along_b(da):
            return pass_on(block(da, 0), peer(0, 1)), pass_on(block(da, 0), peer(0, -1))

        right = pass_on(block(0, 0), peer(1, 0))
        left = pass_on(block(0, 0), peer(-1, 0))
        pairs = {0: along_b(0)}
        more = {}

        def along_b_more(da):
            landed(pairs[da][0], block(da, -1))
            first = pass_on(block(da, -1, 0), peer(0, 1))
            landed(pairs[da][1], block(da, 1))
            more[da] = first, pass_on(block(da, 1, 1), peer(0, -1))
            decode(at(da, -1), s)
            decode(at(da, 1), s)

        yield
        decode(col, s)
        landed(right, block(-1, 0))
        on_right = pass_on(block(-1, 0, 0), peer(1, 0))
        pairs[-1] = along_b(-1)
        yield
        landed(left, block(1, 0))
        on_left = pass_on(block(1, 0, 1), peer(-1, 0))
        pairs[1] = along_b(1)
        yield
        along_b_more(0)
        yield
        landed(on_right, block(2, 0, 0))
        landed(on_left, block(2, 0, 1))
        pairs[2] = along_b(2)
        for da in (-1, 1, 2):
            decode(at(da, 0), s)
        for da in (-1, 1, 2):
            yield
            along_b_more(da)
        for da in (0, -1, 1, 2):
            yield
            landed(more[da][0], block(da, 2, 0))
            landed(more[da][1], block(da, 2, 1))
            decode(at(da, 2), s)

    def look(s, first, out):
        acc = None
        for p in range(s * N, s * N + N):
            some = counts[pl.ds(pl.multiple_of(first, 256), 256), p * 512 : (p + 1) * 512]
            for k in range(2):
                term = lax.dot_general(
                    some, wide[k, p].reshape(256, 512), NT, preferred_element_type=F32
                )
                acc = term if acc is None else acc + term
        if s == 0:
            out[...] = acc
        else:
            out[...] += acc

    renew(0, 8)
    units[col] = (jnp.maximum(unit[...], 1e-30) * (1.008 / 32000.0)).astype(BF16)
    unit[...] = 1.0 / units[col].astype(F32)
    encode(0)
    one, two = widen(0), widen(1)
    next(one)
    k_unit = [go(units.at[col], units.at[col], plane(d)) for d in range(1, 16)]
    encode(1)
    next(two)
    k_old = go(fresh, old_in, twin)
    for d in range(8):
        landed(k_hand[d], all_synced.at[plus(z, -d, 8) * 2 + 1 - core])
    next(one)
    next(one)
    next(two)
    next(two)
    for d in range(1, 16):
        landed(k_unit[d - 1], units.at[plus(col, -d, 16)])
    next(one)
    next(one)
    next(two)
    next(one)
    next(one)
    next(two)
    for _ in one:
        pass
    chunks = [(for_twin, 1024, m) for m in range(4)] + [(pooled, 0, m) for m in range(4)]
    for out, first, m in chunks:
        look(0, first + m * 256, out.at[m])
        next(two, None)
    for _ in two:
        pass

    k_pool = []
    for m in range(4):
        look(1, 1024 + m * 256, for_twin.at[m])
        k_pool.append(go(for_twin.at[m], pooled_in.at[m], twin))

    @pl.loop(0, 4)
    def _(m):
        look(1, m * 256, pooled.at[m])

    for m in range(4):
        landed(k_pool[m], pooled_in.at[m])

    for load in loads[2:]:
        load.wait()
    both = [(pooled[m] + pooled_in[m]).astype(BF16) for m in range(4)]
    x0 = jnp.concatenate(
        [both[f // 2][f % 2 * 128 : f % 2 * 128 + 128] for f in range(8)], axis=1
    )
    low = jnp.dot(x0, down[...], preferred_element_type=F32).astype(BF16)
    gate = jnp.dot(low, up[...], preferred_element_type=F32) + cross_bias[...]
    wide0 = x0.astype(F32)
    x1 = (wide0 * gate + wide0).astype(BF16)
    pre = jnp.dot(x1, top[...], preferred_element_type=F32) + top_bias[...]
    sig = jax.nn.sigmoid(pre)
    hidden = (pre * sig).astype(BF16).astype(F32)
    weight = out_weight[...].astype(F32).reshape(1, 1024)
    logit = jnp.sum(hidden * weight, axis=1, keepdims=True)
    across = jnp.broadcast_to(logit, (128, 128)).T
    logits[...] = across[0:1, :]
    dlogit = jax.nn.sigmoid(across) - label[...].astype(F32)
    dlogit = dlogit.T[:, 0:1]
    slope = sig * (1.0 + pre * (1.0 - sig))
    dhidden = (dlogit * weight * slope).astype(BF16)
    dx1 = lax.dot_general(dhidden, top[...], NT, preferred_element_type=F32)
    dgate = (dx1 * wide0).astype(BF16)
    dlow = lax.dot_general(dgate, up[...], NT, preferred_element_type=F32).astype(BF16)
    k_back = []
    for c in range(4):
        lanes = slice(c * 512, (c + 1) * 512)
        dx0 = dx1[:, lanes] * (gate[:, lanes] + 1.0) + lax.dot_general(
            dlow, down[lanes, :], NT, preferred_element_type=F32
        )
        for f in range(2):
            back[c, :, f * 128 : (f + 1) * 128] = dx0[:, f * 256 : (f + 1) * 256].T.astype(BF16)
        k_back.append(go(back.at[c], back.at[4 + c], twin))

    for c in range(4):
        landed(k_back[c], back.at[4 + c])

    def slopes(lo, hi):
        @pl.loop(lo, hi)
        def _(p):
            lanes = pl.ds(pl.multiple_of(p * 512, 512), 512)
            acc = None
            for c in range(8):
                term = jnp.dot(
                    back[c], counts[c * 256 : (c + 1) * 256, lanes], preferred_element_type=F32
                )
                acc = term if acc is None else acc + term
            grads[:, p] = acc.astype(BF16).reshape(16, 16, 512)

    def add(ref, other):
        ref[...] = (ref[...].astype(F32) + other[...].astype(F32)).astype(BF16)

    order = [(da, db) for da in (2, 1, -1, 0) for db in (2, 1, -1, 0)]

    def narrow(s):
        whole = pl.ds(s * N, N)
        lo, hi = pl.ds(s * N, N // 2), pl.ds(s * N + N // 2, N // 2)
        few = pl.ds(s * N // 2, N // 2)
        ways = [{} for _ in range(4)]
        last = {}

        def first_part(i):
            for j in range(4):
                k = i * 4 + j
                where = at(*order[k])
                if j == 0:
                    ways[i][0] = go(grads.at[where, lo], fwd_in.at[i, 0, few], peer(0, 1))
                    ways[i][1] = go(grads.at[where, hi], fwd_in.at[i, 1, few], peer(0, -1))
                if j == 1:
                    ways[i][2] = go(grads.at[where, hi], side_in.at[i, 0, hi], peer(0, 1))
                if j == 2:
                    ways[i][3] = go(grads.at[where, lo], side_in.at[i, 1, lo], peer(0, -1))

        def second_part(i):
            landed(ways[i][0], fwd_in.at[i, 0, few])
            add(grads.at[at(*order[i * 4 + 1]), lo], fwd_in.at[i, 0, few])
            ways[i][4] = go(grads.at[at(*order[i * 4 + 1]), lo], side_in.at[i, 0, lo], peer(0, 1))
            landed(ways[i][1], fwd_in.at[i, 1, few])
            add(grads.at[at(*order[i * 4 + 2]), hi], fwd_in.at[i, 1, few])
            ways[i][5] = go(grads.at[at(*order[i * 4 + 2]), hi], side_in.at[i, 1, hi], peer(0, -1))

        def third_part(i):
            landed(ways[i][2], side_in.at[i, 0, hi])
            landed(ways[i][3], side_in.at[i, 1, lo])
            landed(ways[i][4], side_in.at[i, 0, lo])
            landed(ways[i][5], side_in.at[i, 1, hi])
            where = at(*order[i * 4 + 3])
            grads[where, whole] = (
                grads[where, whole].astype(F32)
                + side_in[i, 0, whole].astype(F32)
                + side_in[i, 1, whole].astype(F32)
            ).astype(BF16)

        def last_axis(i):
            where = at(*order[i * 4 + 3])
            if i == 0:
                last[0] = go(grads.at[where, lo], far_in.at[0, few], peer(1, 0))
                last[1] = go(grads.at[where, hi], far_in.at[1, few], peer(-1, 0))
            if i == 1:
                last[2] = go(grads.at[where, hi], lane_in.at[0, hi], peer(1, 0))
                landed(last[0], far_in.at[0, few])
                add(grads.at[where, lo], far_in.at[0, few])
                last[4] = go(grads.at[where, lo], lane_in.at[0, lo], peer(1, 0))
            if i == 2:
                last[3] = go(grads.at[where, lo], lane_in.at[1, lo], peer(-1, 0))
                landed(last[1], far_in.at[1, few])
                add(grads.at[where, hi], far_in.at[1, few])
                last[5] = go(grads.at[where, hi], lane_in.at[1, hi], peer(-1, 0))

        def begin():
            for i in range(4):
                first_part(i)

        def more(*parts):
            for i in parts:
                second_part(i)

        def turn(i):
            third_part(i)
            last_axis(i)

        def finish():
            turn(3)
            landed(last[2], lane_in.at[0, hi])
            landed(last[3], lane_in.at[1, lo])
            landed(last[4], lane_in.at[0, lo])
            landed(last[5], lane_in.at[1, hi])
            ring_out[whole] = (
                grads[col, whole].astype(F32)
                + lane_in[0, whole].astype(F32)
                + lane_in[1, whole].astype(F32)
            ).astype(BF16)

        return begin, more, turn, finish

    slopes(0, 4)
    begin0, more0, turn0, finish0 = narrow(0)
    begin1, more1, turn1, finish1 = narrow(1)
    begin0()
    slopes(4, 6)
    more0(0, 1)
    slopes(6, 8)
    begin1()
    more0(2, 3)
    turn0(0)
    turn0(1)
    more1(0, 1)
    turn0(2)
    more1(2, 3)
    turn1(0)
    turn1(1)
    finish0()
    turn1(2)
    finish1()

    k_ring = [go(ring_out.at[plus(z, d, 8)], ring_in.at[d], ring(d)) for d in range(1, 8)]
    demoted(0, 16)
    grad = ring_out[z].astype(F32)
    for d in range(1, 8):
        landed(k_ring[d - 1], ring_in.at[d])
        grad = grad + ring_in[d].astype(F32)
    square = jnp.sum(grad * grad, axis=0, keepdims=True)
    square = [square[:, i * 128 : (i + 1) * 128] for i in range(4)]
    squares[col] = jnp.concatenate(square + square, axis=0)
    k_sq = [go(squares.at[col], squares.at[col], plane(d)) for d in range(1, 16)]
    all_grads[grp] = grad.astype(BF16)
    k_all = [go(all_grads.at[grp], all_grads.at[grp], ring(d)) for d in range(1, 8)]
    k_hand = [go(all_grads.at[grp], all_grads.at[grp], twin)]
    table_out(0, 9)
    for d in range(1, 16):
        landed(k_sq[d - 1], squares.at[plus(col, -d, 16)])
    before = accum[pl.ds(core * 32 + z * 4, 4), :]
    sums[grp] = jnp.concatenate([before, before], axis=0) + jnp.sum(squares[...], axis=0) / E
    k_sum = [go(sums.at[grp], sums.at[grp], group(d)) for d in range(1, 16)]
    table_out(9, 16)
    for d in range(1, 8):
        there = all_grads.at[plus(z, -d, 8) * 2 + core]
        landed(k_all[d - 1], there)
        k_hand.append(go(there, there, twin))
    for d in range(8):
        landed(k_hand[d], all_grads.at[plus(z, -d, 8) * 2 + 1 - core])
    for d in range(1, 16):
        landed(k_sum[d - 1], sums.at[plus(grp, -d, 16)])
    landed(k_old, old_in)
    for h in range(2):
        for p in range(8):
            new_accum[h * 32 + p * 4 : h * 32 + p * 4 + 4, :] = sums[p * 2 + h, 0:4, :]

        @pl.loop(0, 8)
        def _(p):
            g = p * 2 + h
            for i in range(4):
                lanes = pl.ds(pl.multiple_of(h * 4096 + p * 512 + i * 128, 128), 128)
                inner = slice(i * 128, (i + 1) * 128)
                scale = STEP / jnp.sqrt(sums[g, i : i + 1, :] + EPS)
                old = jnp.where(core == h, fresh[p, :, inner], old_in[p, :, inner])
                new_hot[:, lanes] = old - all_grads[g, :, inner].astype(F32) * scale

    for copy in started:
        copy.wait_send()


def step(*args):
    dma = pltpu.SemaphoreType.DMA
    v = pltpu.VMEM
    return pl.pallas_call(
        step_kernel,
        out_shape=[
            jax.ShapeDtypeStruct((16, 8192), F32),
            jax.ShapeDtypeStruct((16, 8192), F32),
            jax.ShapeDtypeStruct((64, 128), F32),
            jax.ShapeDtypeStruct((1, 128), F32),
        ],
        in_specs=[VMEM] * 11 + [ANY] * 5,
        out_specs=[VMEM] * 4,
        scratch_shapes=[
            v((2048, 512), BF16),
            v((512, 2048), BF16),
            v((2048, 1024), BF16),
            v((4, 8, 128), I32),
            v((4, 8, 128), I32),
            v((2, 8, 16, 512), F32),
            v((8, 16, 512), F32),
            v((8, 16, 512), F32),
            v((8, 16, 512), F32),
            v((16, 512), F32),
            v((16, 16, 128), F32),
            v((16, 16, 128), F32),
            v((16, 16, 128), F32),
            v((16, 128), I32),
            v((16, 8, 128), I32),
            v((32, 128), I32),
            v((2, 4, 8, 128), I32),
            v((16, 16, 512), F32),
            v((16, 8, 16, 512), I16),
            v((8, 16, 512), F32),
            v((8, 16, 512), F32),
            v((32, 128), F32),
            v((16, 32, 128), BF16),
            v((32, 128), F32),
            v((2, 8, 16, 16, 512), BF16),
            v((4, 2048, 128), I16),
            v((2048, 4096), BF16),
            v((4, 256, 256), F32),
            v((4, 256, 256), F32),
            v((4, 256, 256), F32),
            v((8, 256, 256), BF16),
            v((16, 8, 16, 512), BF16),
            v((16, 16, 128), F32),
            v((64, 128), I32),
            v((4, 2, 4, 16, 512), BF16),
            v((4, 2, 8, 16, 512), BF16),
            v((2, 8, 16, 512), BF16),
            v((2, 4, 16, 512), BF16),
            v((8, 16, 512), BF16),
            v((8, 16, 512), BF16),
            v((16, 16, 512), BF16),
            v((16, 8, 128), F32),
            v((16, 8, 128), F32),
            dma((5,)),
            dma((N_SEM,)),
            dma((N_SEM,)),
        ],
        compiler_params=pltpu.CompilerParams(
            collective_id=0, has_side_effects=True, vmem_limit_bytes=62 << 20
        ),
    )(*args)


def hand_out_kernel(*refs):
    n = len(refs) // 2
    for i in range(n):
        refs[n + i][...] = refs[i][...]


def hand_out(*arrays):
    return pl.pallas_call(
        hand_out_kernel,
        out_shape=[jax.ShapeDtypeStruct(a.shape, a.dtype) for a in arrays],
        in_specs=[VMEM] * len(arrays),
        out_specs=[VMEM] * len(arrays),
    )(*arrays)


def per_device(
    table, hot, accum, pending, slot_ids, demote_ids, promote_ids, bag_rows, bag_mask, labels,
    cross_down, cross_up, cross_bias, top_weight, top_bias, out_weight,
):
    outputs = step(
        pending[0], table, hot, accum.reshape(64, 128), slot_ids.reshape(16, 128),
        demote_ids.reshape(16, 128), promote_ids.reshape(16, 128), labels, cross_bias[None],
        top_bias[None], out_weight, bag_rows, bag_mask, cross_down, cross_up, top_weight,
    )
    new_table, new_hot, new_accum, logits = hand_out(*outputs)
    return new_table, new_hot, new_accum.reshape(8192), logits


def solution(mesh):
    return jax.shard_map(
        per_device,
        mesh=mesh,
        in_specs=(
            P("col", "grp"), P("col", None), P(), P("grp", "col", None), P(), P(), P(),
            P(None, None, "grp"), P(None, None, "grp"), P("col", "grp"),
            P(), P(), P(), P(), P(), P(),
        ),
        out_specs=(P("col", "grp"), P("col", None), P(), P("col", "grp")),
        check_vma=False,
    )
```

```python
import jax
import jax.numpy as jnp
from jax import lax
from jax.experimental import pallas as pl
from jax.experimental.pallas import tpu as pltpu
from jax.sharding import PartitionSpec as P

E = 256
STEP = 0.2
EPS = 1e-06
MESH = pl.DeviceIdType.MESH
F32 = jnp.float32
BF16 = jnp.bfloat16
I16 = jnp.int16
I32 = jnp.int32
VMEM = pl.BlockSpec(memory_space=pltpu.VMEM)
ANY = pl.BlockSpec(memory_space=pl.ANY)
NT = (((1,), (1,)), ((), ()))
N_SEM = 288
N = 4


def plus(a, d, n):
    return lax.rem(a + d + n, n)


def column(core, a, b):
    return jnp.where(core == 0, b * 4 + a, a * 4 + b)


def pick_lanes(idx, tiles, read):
    idx = jnp.broadcast_to(idx, (8, 128))
    low = idx & 127
    high = idx >> 7
    top = jnp.zeros((8, 128), F32)
    bottom = jnp.zeros((8, 128), F32)
    for t in range(tiles):
        hit = high == t
        a, b = read(t)
        top = jnp.where(hit, jnp.take_along_axis(a, low, axis=1, mode="promise_in_bounds"), top)
        bottom = jnp.where(
            hit, jnp.take_along_axis(b, low, axis=1, mode="promise_in_bounds"), bottom
        )
    return jnp.concatenate([top, bottom], axis=0)


def split(tile):
    tile = tile.astype(F32)
    return tile[0:8], tile[8:16]


def upright(row):
    return jnp.broadcast_to(row, (128, 128)).T


def step_kernel(
    pending, table, hot, accum, slot, demote, promote, label, cross_bias, top_bias, out_weight,
    bag_rows, bag_mask, down_hbm, up_hbm, top_hbm,
    new_table, new_hot, new_accum, logits,
    down, up, top, rows_in, mask_in,
    mine, from_twin, reduced, from_ring, synced, fetched, fetched_in, arrived, match, best, slot_from,
    bags, all_synced, full, fresh, old_in, unit, units, unit_of, wide, bag_col, counts, pooled, for_twin, pooled_in, back, grads,
    x0_ref, x1_ref, gate_ref, dx1_ref, pre_ref,    evicted, home, fwd_in, side_in, lane_in, far_in, ring_out, ring_in, all_grads, squares, sums,
    load_sem, send_sem, recv_sem,
):
    col = lax.axis_index("col")
    grp = lax.axis_index("grp")
    z, core = lax.div(grp, 2), lax.rem(grp, 2)
    x, y = lax.rem(col, 4), lax.div(col, 4)
    a, b = jnp.where(core == 0, x, y), jnp.where(core == 0, y, x)
    twin = (col, grp + 1 - 2 * core)
    started = []
    used = [0]

    def at(da, db):
        return column(core, plus(a, da, 4), plus(b, db, 4))

    def peer(da, db):
        return (at(da, db), grp)

    def ring(d):
        return (col, plus(z, d, 8) * 2 + core)

    def group(d):
        return (col, plus(grp, d, 16))

    def plane(d):
        return (plus(col, d, 16), grp)

    def go(src, dst, to):
        k = used[0]
        used[0] += 1
        copy = pltpu.make_async_remote_copy(
            src_ref=src, dst_ref=dst, send_sem=send_sem.at[k], recv_sem=recv_sem.at[k],
            device_id=to, device_id_type=MESH,
        )
        copy.start()
        started.append(copy)
        return k

    def landed(k, dst):
        pltpu.make_async_remote_copy(
            src_ref=dst, dst_ref=dst, send_sem=send_sem.at[k], recv_sem=recv_sem.at[k],
            device_id=twin, device_id_type=MESH,
        ).wait_recv()

    loads = [
        pltpu.make_async_copy(src, dst, load_sem.at[i])
        for i, (src, dst) in enumerate(
            (
                (bag_rows.at[:, :, pl.ds(pl.multiple_of(col * 128, 128), 128)], rows_in),
                (bag_mask.at[:, :, pl.ds(pl.multiple_of(col * 128, 128), 128)], mask_in),
                (down_hbm, down),
                (up_hbm, up),
                (top_hbm, top),
            )
        )
    ]
    for load in loads:
        load.start()
    barrier = pltpu.get_barrier_semaphore()
    others = [group(d) for d in range(1, 16)] + [plane(d) for d in range(1, 16)]
    for other in others:
        pl.semaphore_signal(barrier, inc=1, device_id=other, device_id_type=MESH)

    def lanes_of(h, p):
        return pl.ds(pl.multiple_of(h * 4096 + p * 512, 512), 512)

    @pl.loop(0, 16)
    def _(i):
        h, p = lax.div(i, 8), lax.rem(i, 8)
        mine[h, p] = pending[:, lanes_of(h, p)]

    best[...] = jnp.full_like(best, -1)

    @pl.loop(0, 16)
    def _(t):
        dem, slo = upright(demote[pl.ds(t, 1), :]), upright(slot[pl.ds(t, 1), :])
        for j in range(16):
            hit = jnp.where(dem == promote[j : j + 1, :], slo, -1)
            best[j] = jnp.maximum(best[j], jnp.max(hit.reshape(16, 8, 128), axis=0))

    for j in range(16):
        match[j : j + 1, :] = jnp.max(best[j], axis=0, keepdims=True)

    @pl.loop(0, 16)
    def _(t):
        idx = promote[pl.ds(t, 1), :] - grp * 8192
        idx = jnp.where((match[pl.ds(t, 1), :] < 0) & (idx >= 0) & (idx < 8192), idx, -1)
        fetched[t] = pick_lanes(
            idx, 64, lambda s: split(table[:, s * 128 : (s + 1) * 128])
        )

    loads[0].wait()
    loads[1].wait()
    bags[0] = jnp.where(mask_in[...] > 0, rows_in[...], -1)
    pl.semaphore_wait(barrier, len(others))

    k_twin = go(mine.at[1 - core], from_twin, twin)

    k_bags = go(bags.at[0], bags.at[1], twin)

    def stand(which):
        @pl.loop(0, 32)
        def _(i):
            l, f = lax.div(i, 8), lax.rem(i, 8)
            row = upright(bags[which, l, pl.ds(f, 1), :] - core * 4096)
            bag_col[l, pl.ds(pl.multiple_of(which * 1024 + f * 128, 128), 128), :] = row.astype(I16)

    stand(0)
    landed(k_twin, from_twin)
    reduced[...] = mine[core] + from_twin[...]
    k_ring = [go(reduced.at[plus(z, d, 8)], from_ring.at[d], ring(d)) for d in range(1, 8)]

    def count(lo, hi):
        @pl.loop(lo, hi)
        def _(i):
            r = pl.ds(pl.multiple_of(i * 16, 16), 16)
            lane = lax.broadcasted_iota(I32, (16, 128), 1)
            idx = [bag_col[l, r, :].astype(I32) for l in range(4)]
            low = [jnp.where((v & 127) == lane, 1.0, 0.0).astype(BF16) for v in idx]
            high = [(v >> 7).astype(F32).astype(BF16) for v in idx]
            zero = jnp.zeros((16, 128), BF16)
            for t in range(32):
                acc = None
                for l in range(4):
                    hit = jnp.where(high[l] == BF16(t), low[l], zero)
                    acc = hit if acc is None else acc + hit
                counts[r, t * 128 : (t + 1) * 128] = acc

    def origin(ids, first, places, half_rows):
        ids = ids - first
        lane = ids & 127
        high = ids >> 7
        j = lax.broadcasted_iota(I32, (1, 2048), 1)
        sub = lax.broadcasted_iota(I32, (128, 2048), 0)
        here = sub == lane
        major = jnp.where(here, (j >> 7).astype(F32), 0.0).astype(BF16)
        minor = jnp.where(here, (j & 127).astype(F32) + 1.0, 0.0).astype(BF16)
        rows = lax.broadcasted_iota(I32, (half_rows, 2048), 0)
        pick = jnp.where(rows == high, 1.0, 0.0).astype(BF16)
        major = lax.dot_general(pick, major, NT, preferred_element_type=F32)
        minor = lax.dot_general(pick, minor, NT, preferred_element_type=F32)
        return (major * 128.0 + minor).astype(I32) - 1

    def flat(ref):
        return jnp.concatenate([ref[t : t + 1, :] for t in range(16)], axis=1)

    slot_from[...] = origin(flat(slot), core * 4096, 4096, 32)
    home[...] = origin(flat(demote), grp * 8192, 8192, 64)
    count(0, 40)
    total = reduced[z]
    for d in range(1, 8):
        landed(k_ring[d - 1], from_ring.at[d])
        total = total + from_ring[d]
    base = core * 4096 + z * 512
    synced[...] = total + hot[:, pl.ds(pl.multiple_of(base, 512), 512)]

    @pl.loop(0, 16)
    def _(t):
        again = match[pl.ds(t, 1), :] - base
        value = pick_lanes(again, 4, lambda s: split(synced[:, s * 128 : (s + 1) * 128]))
        fetched[t] = value + fetched[t]

    k_fet = [go(fetched.at[plus(grp, d, 16)], fetched_in.at[d], group(d)) for d in range(1, 16)]
    all_synced[grp] = synced[...]
    k_syn = [go(all_synced.at[grp], all_synced.at[grp], ring(d)) for d in range(1, 8)]
    k_hand = [go(all_synced.at[grp], all_synced.at[grp], twin)]
    landed(k_bags, bags.at[1])
    stand(1)
    count(40, 84)
    mine_now = fetched[grp]
    for d in range(1, 16):
        landed(k_fet[d - 1], fetched_in.at[d])
        mine_now = mine_now + fetched_in[d]
    arrived[grp] = mine_now
    k_arr = [go(arrived.at[grp], arrived.at[grp], group(d)) for d in range(1, 16)]
    count(84, 128)
    for d in range(1, 8):
        there = all_synced.at[plus(z, -d, 8) * 2 + core]
        landed(k_syn[d - 1], there)
        k_hand.append(go(there, there, twin))
    for d in range(1, 16):
        landed(k_arr[d - 1], arrived.at[plus(grp, -d, 16)])

    def renew(lo, hi):
        @pl.loop(lo, hi)
        def _(p):
            for i in range(4):
                idx = slot_from[pl.ds(p * 4 + i, 1), :]
                lanes = slice(i * 128, (i + 1) * 128)
                picked = pick_lanes(idx, 16, lambda s: split(arrived[s]))
                old = all_synced[p * 2 + core, :, lanes]
                value = jnp.where(jnp.broadcast_to(idx, (16, 128)) >= 0, picked, old)
                fresh[p, :, lanes] = value
                unit[pl.ds(p * 4 + i, 1), :] = jnp.max(jnp.abs(value), axis=0, keepdims=True)

    def encode():
        units[col] = (jnp.maximum(unit[...], 1e-30) * (1.008 / 32000.0)).astype(BF16)
        unit[...] = 1.0 / units[col].astype(F32)

        @pl.loop(0, 8)
        def _(p):
            for i in range(4):
                lanes = slice(i * 128, (i + 1) * 128)
                code = jnp.round(fresh[p, :, lanes] * unit[pl.ds(p * 4 + i, 1), :])
                full[col, p, :, lanes] = code.astype(I32).astype(I16)

    def decode(c):
        unit_of[...] = units[c].astype(F32)

        @pl.loop(0, 8)
        def _(p):
            for i in range(4):
                lanes = slice(i * 128, (i + 1) * 128)
                value = full[c, p, :, lanes].astype(I32).astype(F32)
                value = value * unit_of[pl.ds(p * 4 + i, 1), :]
                high = value.astype(BF16)
                wide[0, p, c, :, lanes] = high
                wide[1, p, c, :, lanes] = (value - high.astype(F32)).astype(BF16)

    def demoted(lo, hi):
        @pl.loop(lo, hi)
        def _(t):
            evicted[t] = pick_lanes(
                slot[pl.ds(t, 1), :], 64,
                lambda s: split(
                    all_synced[
                        (s % 32 // 4) * 2 + s // 32, :, (s % 4) * 128 : (s % 4 + 1) * 128
                    ]
                ),
            )

    def table_out(lo, hi):
        @pl.loop(lo, hi)
        def _(q):
            for u in range(4):
                lanes = pl.ds(pl.multiple_of(q * 512 + u * 128, 128), 128)
                idx = home[pl.ds(q * 4 + u, 1), :]
                picked = pick_lanes(idx, 16, lambda s: (evicted[s, 0:8, :], evicted[s, 8:16, :]))
                new_table[:, lanes] = jnp.where(
                    jnp.broadcast_to(idx, (16, 128)) >= 0, picked, table[:, lanes]
                )

    def widen():
        half = pl.ds(0, 4), pl.ds(4, 4)

        def block(da, db, which=None):
            ref = full.at[at(da, db)]
            return ref if which is None else ref.at[half[which]]

        def pass_on(ref, to):
            return go(ref, ref, to)

        def along_b(da):
            return pass_on(block(da, 0), peer(0, 1)), pass_on(block(da, 0), peer(0, -1))

        right = pass_on(block(0, 0), peer(1, 0))
        left = pass_on(block(0, 0), peer(-1, 0))
        pairs = {0: along_b(0)}
        more = {}

        def along_b_more(da):
            landed(pairs[da][0], block(da, -1))
            first = pass_on(block(da, -1, 0), peer(0, 1))
            landed(pairs[da][1], block(da, 1))
            more[da] = first, pass_on(block(da, 1, 1), peer(0, -1))
            decode(at(da, -1))
            decode(at(da, 1))

        yield
        decode(col)
        landed(right, block(-1, 0))
        on_right = pass_on(block(-1, 0, 0), peer(1, 0))
        pairs[-1] = along_b(-1)
        yield
        landed(left, block(1, 0))
        on_left = pass_on(block(1, 0, 1), peer(-1, 0))
        pairs[1] = along_b(1)
        yield
        along_b_more(0)
        yield
        landed(on_right, block(2, 0, 0))
        landed(on_left, block(2, 0, 1))
        pairs[2] = along_b(2)
        for da in (-1, 1, 2):
            decode(at(da, 0))
        for da in (-1, 1, 2):
            yield
            along_b_more(da)
        for da in (0, -1, 1, 2):
            yield
            landed(more[da][0], block(da, 2, 0))
            landed(more[da][1], block(da, 2, 1))
            decode(at(da, 2))

    def look(first, out):
        acc = None
        for p in range(8):
            some = counts[pl.ds(pl.multiple_of(first, 256), 256), p * 512 : (p + 1) * 512]
            for k in range(2):
                term = lax.dot_general(
                    some, wide[k, p].reshape(256, 512), NT, preferred_element_type=F32
                )
                acc = term if acc is None else acc + term
        out[...] = acc

    renew(0, 8)
    encode()
    travel = widen()
    next(travel)
    k_unit = [go(units.at[col], units.at[col], plane(d)) for d in range(1, 16)]
    k_old = go(fresh, old_in, twin)
    for d in range(8):
        landed(k_hand[d], all_synced.at[plus(z, -d, 8) * 2 + 1 - core])
    next(travel)
    next(travel)
    for d in range(1, 16):
        landed(k_unit[d - 1], units.at[plus(col, -d, 16)])
    for _ in travel:
        pass

    k_pool = []

    @pl.loop(0, 4)
    def _(m):
        look(1024 + m * 256, for_twin.at[m])

    for m in range(4):
        k_pool.append(go(for_twin.at[m], pooled_in.at[m], twin))

    @pl.loop(0, 4)
    def _(m):
        look(m * 256, pooled.at[m])

    for m in range(4):
        landed(k_pool[m], pooled_in.at[m])

    for load in loads[2:]:
        load.wait()
    both = [(pooled[m] + pooled_in[m]).astype(BF16) for m in range(4)]
    x0_ref[...] = jnp.concatenate(
        [both[f // 2][f % 2 * 128 : f % 2 * 128 + 128] for f in range(8)], axis=1
    )
    low = jnp.dot(x0_ref[...], down[...], preferred_element_type=F32).astype(BF16)

    def lanes_at(i, size):
        return pl.ds(pl.multiple_of(i * size, size), size)

    @pl.loop(0, 4)
    def _(i):
        lanes = lanes_at(i, 512)
        gate = jnp.dot(low, up[:, lanes], preferred_element_type=F32) + cross_bias[:, lanes]
        gate_ref[:, lanes] = gate
        wide0 = x0_ref[:, lanes].astype(F32)
        x1_ref[:, lanes] = (wide0 * gate + wide0).astype(BF16)

    @pl.loop(0, 4)
    def _(i):
        lanes = lanes_at(i, 256)
        pre_ref[:, lanes] = (
            jnp.dot(x1_ref[...], top[:, lanes], preferred_element_type=F32) + top_bias[:, lanes]
        )

    pre = pre_ref[...]
    sig = jax.nn.sigmoid(pre)
    hidden = (pre * sig).astype(BF16).astype(F32)
    weight = out_weight[...].astype(F32).reshape(1, 1024)
    logit = jnp.sum(hidden * weight, axis=1, keepdims=True)
    across = jnp.broadcast_to(logit, (128, 128)).T
    logits[...] = across[0:1, :]
    dlogit = jax.nn.sigmoid(across) - label[...].astype(F32)
    dlogit = dlogit.T[:, 0:1]
    slope = sig * (1.0 + pre * (1.0 - sig))
    dhidden = (dlogit * weight * slope).astype(BF16)

    @pl.loop(0, 4)
    def _(i):
        lanes = lanes_at(i, 512)
        dx1 = lax.dot_general(dhidden, top[lanes, :], NT, preferred_element_type=F32)
        dx1_ref[:, lanes] = dx1
        x1_ref[:, lanes] = (dx1 * x0_ref[:, lanes].astype(F32)).astype(BF16)

    dlow = lax.dot_general(x1_ref[...], up[...], NT, preferred_element_type=F32).astype(BF16)
    k_back = []
    for c in range(4):
        lanes = slice(c * 512, (c + 1) * 512)
        dx0 = dx1_ref[:, lanes] * (gate_ref[:, lanes] + 1.0) + lax.dot_general(
            dlow, down[lanes, :], NT, preferred_element_type=F32
        )
        for f in range(2):
            back[c, :, f * 128 : (f + 1) * 128] = dx0[:, f * 256 : (f + 1) * 256].T.astype(BF16)
        k_back.append(go(back.at[c], back.at[4 + c], twin))

    for c in range(4):
        landed(k_back[c], back.at[4 + c])

    def slopes(lo, hi):
        @pl.loop(lo, hi)
        def _(p):
            lanes = pl.ds(pl.multiple_of(p * 512, 512), 512)
            acc = None
            for c in range(8):
                term = jnp.dot(
                    back[c], counts[c * 256 : (c + 1) * 256, lanes], preferred_element_type=F32
                )
                acc = term if acc is None else acc + term
            grads[:, p] = acc.astype(BF16).reshape(16, 16, 512)

    def add(ref, other):
        ref[...] = (ref[...].astype(F32) + other[...].astype(F32)).astype(BF16)

    order = [(da, db) for da in (2, 1, -1, 0) for db in (2, 1, -1, 0)]

    def narrow(s):
        whole = pl.ds(s * N, N)
        lo, hi = pl.ds(s * N, N // 2), pl.ds(s * N + N // 2, N // 2)
        few = pl.ds(s * N // 2, N // 2)
        ways = [{} for _ in range(4)]
        last = {}

        def first_part(i):
            for j in range(4):
                k = i * 4 + j
                where = at(*order[k])
                if j == 0:
                    ways[i][0] = go(grads.at[where, lo], fwd_in.at[i, 0, few], peer(0, 1))
                    ways[i][1] = go(grads.at[where, hi], fwd_in.at[i, 1, few], peer(0, -1))
                if j == 1:
                    ways[i][2] = go(grads.at[where, hi], side_in.at[i, 0, hi], peer(0, 1))
                if j == 2:
                    ways[i][3] = go(grads.at[where, lo], side_in.at[i, 1, lo], peer(0, -1))

        def second_part(i):
            landed(ways[i][0], fwd_in.at[i, 0, few])
            add(grads.at[at(*order[i * 4 + 1]), lo], fwd_in.at[i, 0, few])
            ways[i][4] = go(grads.at[at(*order[i * 4 + 1]), lo], side_in.at[i, 0, lo], peer(0, 1))
            landed(ways[i][1], fwd_in.at[i, 1, few])
            add(grads.at[at(*order[i * 4 + 2]), hi], fwd_in.at[i, 1, few])
            ways[i][5] = go(grads.at[at(*order[i * 4 + 2]), hi], side_in.at[i, 1, hi], peer(0, -1))

        def third_part(i):
            landed(ways[i][2], side_in.at[i, 0, hi])
            landed(ways[i][3], side_in.at[i, 1, lo])
            landed(ways[i][4], side_in.at[i, 0, lo])
            landed(ways[i][5], side_in.at[i, 1, hi])
            where = at(*order[i * 4 + 3])
            grads[where, whole] = (
                grads[where, whole].astype(F32)
                + side_in[i, 0, whole].astype(F32)
                + side_in[i, 1, whole].astype(F32)
            ).astype(BF16)

        def last_axis(i):
            where = at(*order[i * 4 + 3])
            if i == 0:
                last[0] = go(grads.at[where, lo], far_in.at[0, few], peer(1, 0))
                last[1] = go(grads.at[where, hi], far_in.at[1, few], peer(-1, 0))
            if i == 1:
                last[2] = go(grads.at[where, hi], lane_in.at[0, hi], peer(1, 0))
                landed(last[0], far_in.at[0, few])
                add(grads.at[where, lo], far_in.at[0, few])
                last[4] = go(grads.at[where, lo], lane_in.at[0, lo], peer(1, 0))
            if i == 2:
                last[3] = go(grads.at[where, lo], lane_in.at[1, lo], peer(-1, 0))
                landed(last[1], far_in.at[1, few])
                add(grads.at[where, hi], far_in.at[1, few])
                last[5] = go(grads.at[where, hi], lane_in.at[1, hi], peer(-1, 0))

        def begin():
            for i in range(4):
                first_part(i)

        def more(*parts):
            for i in parts:
                second_part(i)

        def turn(i):
            third_part(i)
            last_axis(i)

        def finish():
            turn(3)
            landed(last[2], lane_in.at[0, hi])
            landed(last[3], lane_in.at[1, lo])
            landed(last[4], lane_in.at[0, lo])
            landed(last[5], lane_in.at[1, hi])
            ring_out[whole] = (
                grads[col, whole].astype(F32)
                + lane_in[0, whole].astype(F32)
                + lane_in[1, whole].astype(F32)
            ).astype(BF16)

        return begin, more, turn, finish

    slopes(0, 4)
    begin0, more0, turn0, finish0 = narrow(0)
    begin1, more1, turn1, finish1 = narrow(1)
    begin0()
    slopes(4, 6)
    more0(0, 1)
    slopes(6, 8)
    begin1()
    more0(2, 3)
    turn0(0)
    turn0(1)
    more1(0, 1)
    turn0(2)
    more1(2, 3)
    turn1(0)
    turn1(1)
    finish0()
    turn1(2)
    finish1()

    k_ring = [go(ring_out.at[plus(z, d, 8)], ring_in.at[d], ring(d)) for d in range(1, 8)]
    demoted(0, 16)
    grad = ring_out[z].astype(F32)
    for d in range(1, 8):
        landed(k_ring[d - 1], ring_in.at[d])
        grad = grad + ring_in[d].astype(F32)
    square = jnp.sum(grad * grad, axis=0, keepdims=True)
    square = [square[:, i * 128 : (i + 1) * 128] for i in range(4)]
    squares[col] = jnp.concatenate(square + square, axis=0)
    k_sq = [go(squares.at[col], squares.at[col], plane(d)) for d in range(1, 16)]
    all_grads[grp] = grad.astype(BF16)
    k_all = [go(all_grads.at[grp], all_grads.at[grp], ring(d)) for d in range(1, 8)]
    k_hand = [go(all_grads.at[grp], all_grads.at[grp], twin)]
    table_out(0, 9)
    for d in range(1, 16):
        landed(k_sq[d - 1], squares.at[plus(col, -d, 16)])
    before = accum[pl.ds(core * 32 + z * 4, 4), :]
    sums[grp] = jnp.concatenate([before, before], axis=0) + jnp.sum(squares[...], axis=0) / E
    k_sum = [go(sums.at[grp], sums.at[grp], group(d)) for d in range(1, 16)]
    table_out(9, 16)
    for d in range(1, 8):
        there = all_grads.at[plus(z, -d, 8) * 2 + core]
        landed(k_all[d - 1], there)
        k_hand.append(go(there, there, twin))
    for d in range(8):
        landed(k_hand[d], all_grads.at[plus(z, -d, 8) * 2 + 1 - core])
    for d in range(1, 16):
        landed(k_sum[d - 1], sums.at[plus(grp, -d, 16)])
    landed(k_old, old_in)
    for h in range(2):
        for p in range(8):
            new_accum[h * 32 + p * 4 : h * 32 + p * 4 + 4, :] = sums[p * 2 + h, 0:4, :]

        @pl.loop(0, 8)
        def _(p):
            g = p * 2 + h
            for i in range(4):
                lanes = pl.ds(pl.multiple_of(h * 4096 + p * 512 + i * 128, 128), 128)
                inner = slice(i * 128, (i + 1) * 128)
                scale = STEP / jnp.sqrt(sums[g, i : i + 1, :] + EPS)
                old = jnp.where(core == h, fresh[p, :, inner], old_in[p, :, inner])
                new_hot[:, lanes] = old - all_grads[g, :, inner].astype(F32) * scale

    for copy in started:
        copy.wait_send()


def step(*args):
    dma = pltpu.SemaphoreType.DMA
    v = pltpu.VMEM
    return pl.pallas_call(
        step_kernel,
        out_shape=[
            jax.ShapeDtypeStruct((16, 8192), F32),
            jax.ShapeDtypeStruct((16, 8192), F32),
            jax.ShapeDtypeStruct((64, 128), F32),
            jax.ShapeDtypeStruct((1, 128), F32),
        ],
        in_specs=[VMEM] * 11 + [ANY] * 5,
        out_specs=[VMEM] * 4,
        scratch_shapes=[
            v((2048, 512), BF16),
            v((512, 2048), BF16),
            v((2048, 1024), BF16),
            v((4, 8, 128), I32),
            v((4, 8, 128), I32),
            v((2, 8, 16, 512), F32),
            v((8, 16, 512), F32),
            v((8, 16, 512), F32),
            v((8, 16, 512), F32),
            v((16, 512), F32),
            v((16, 16, 128), F32),
            v((16, 16, 128), F32),
            v((16, 16, 128), F32),
            v((16, 128), I32),
            v((16, 8, 128), I32),
            v((32, 128), I32),
            v((2, 4, 8, 128), I32),
            v((16, 16, 512), F32),
            v((16, 8, 16, 512), I16),
            v((8, 16, 512), F32),
            v((8, 16, 512), F32),
            v((32, 128), F32),
            v((16, 32, 128), BF16),
            v((32, 128), F32),
            v((2, 8, 16, 16, 512), BF16),
            v((4, 2048, 128), I16),
            v((2048, 4096), BF16),
            v((4, 256, 256), F32),
            v((4, 256, 256), F32),
            v((4, 256, 256), F32),
            v((8, 256, 256), BF16),
            v((16, 8, 16, 512), BF16),
            v((128, 2048), BF16),
            v((128, 2048), BF16),
            v((128, 2048), F32),
            v((128, 2048), F32),
            v((128, 1024), F32),
            v((16, 16, 128), F32),
            v((64, 128), I32),
            v((4, 2, 4, 16, 512), BF16),
            v((4, 2, 8, 16, 512), BF16),
            v((2, 8, 16, 512), BF16),
            v((2, 4, 16, 512), BF16),
            v((8, 16, 512), BF16),
            v((8, 16, 512), BF16),
            v((16, 16, 512), BF16),
            v((16, 8, 128), F32),
            v((16, 8, 128), F32),
            dma((5,)),
            dma((N_SEM,)),
            dma((N_SEM,)),
        ],
        compiler_params=pltpu.CompilerParams(
            collective_id=0, has_side_effects=True, vmem_limit_bytes=62 << 20
        ),
    )(*args)


def hand_out_kernel(*refs):
    n = len(refs) // 2
    for i in range(n):
        refs[n + i][...] = refs[i][...]


def hand_out(*arrays):
    return pl.pallas_call(
        hand_out_kernel,
        out_shape=[jax.ShapeDtypeStruct(a.shape, a.dtype) for a in arrays],
        in_specs=[VMEM] * len(arrays),
        out_specs=[VMEM] * len(arrays),
    )(*arrays)


def per_device(
    table, hot, accum, pending, slot_ids, demote_ids, promote_ids, bag_rows, bag_mask, labels,
    cross_down, cross_up, cross_bias, top_weight, top_bias, out_weight,
):
    outputs = step(
        pending[0], table, hot, accum.reshape(64, 128), slot_ids.reshape(16, 128),
        demote_ids.reshape(16, 128), promote_ids.reshape(16, 128), labels, cross_bias[None],
        top_bias[None], out_weight, bag_rows, bag_mask, cross_down, cross_up, top_weight,
    )
    new_table, new_hot, new_accum, logits = hand_out(*outputs)
    return new_table, new_hot, new_accum.reshape(8192), logits


def solution(mesh):
    return jax.shard_map(
        per_device,
        mesh=mesh,
        in_specs=(
            P("col", "grp"), P("col", None), P(), P("grp", "col", None), P(), P(), P(),
            P(None, None, "grp"), P(None, None, "grp"), P("col", "grp"),
            P(), P(), P(), P(), P(), P(),
        ),
        out_specs=(P("col", "grp"), P("col", None), P(), P("col", "grp")),
        check_vma=False,
    )
```

```python
import jax
import jax.numpy as jnp
from jax import lax
from jax.experimental import pallas as pl
from jax.experimental.pallas import tpu as pltpu
from jax.sharding import PartitionSpec as P

E = 256
STEP = 0.2
EPS = 1e-06
MESH = pl.DeviceIdType.MESH
F32 = jnp.float32
BF16 = jnp.bfloat16
I16 = jnp.int16
I32 = jnp.int32
VMEM = pl.BlockSpec(memory_space=pltpu.VMEM)
ANY = pl.BlockSpec(memory_space=pl.ANY)
NT = (((1,), (1,)), ((), ()))
N_SEM = 288
N = 4


def plus(a, d, n):
    return lax.rem(a + d + n, n)


def column(core, a, b):
    return jnp.where(core == 0, b * 4 + a, a * 4 + b)


def pick_lanes(idx, tiles, read):
    idx = jnp.broadcast_to(idx, (8, 128))
    low = idx & 127
    high = idx >> 7
    top = jnp.zeros((8, 128), F32)
    bottom = jnp.zeros((8, 128), F32)
    for t in range(tiles):
        hit = high == t
        a, b = read(t)
        top = jnp.where(hit, jnp.take_along_axis(a, low, axis=1, mode="promise_in_bounds"), top)
        bottom = jnp.where(
            hit, jnp.take_along_axis(b, low, axis=1, mode="promise_in_bounds"), bottom
        )
    return jnp.concatenate([top, bottom], axis=0)


def split(tile):
    tile = tile.astype(F32)
    return tile[0:8], tile[8:16]


def upright(row):
    return jnp.broadcast_to(row, (128, 128)).T


def step_kernel(
    pending, table, hot, accum, slot, demote, promote, label, cross_bias, top_bias, out_weight,
    bag_rows, bag_mask, down_hbm, up_hbm, top_hbm,
    new_table, new_hot, new_accum, logits,
    down, up, top, rows_in, mask_in,
    mine, from_twin, reduced, from_ring, synced, fetched, fetched_in, arrived, match, best, slot_from,
    bags, all_synced, full, fresh, old_in, unit, units, unit_of, wide, bag_col, counts, pooled, for_twin, pooled_in, back, grads,
    x0_ref, x1_ref, gate_ref, dx1_ref, pre_ref,    evicted, home, fwd_in, side_in, lane_in, far_in, ring_out, ring_in, all_grads, squares, sums,
    load_sem, send_sem, recv_sem,
):
    col = lax.axis_index("col")
    grp = lax.axis_index("grp")
    z, core = lax.div(grp, 2), lax.rem(grp, 2)
    x, y = lax.rem(col, 4), lax.div(col, 4)
    a, b = jnp.where(core == 0, x, y), jnp.where(core == 0, y, x)
    twin = (col, grp + 1 - 2 * core)
    started = []
    used = [0]

    def at(da, db):
        return column(core, plus(a, da, 4), plus(b, db, 4))

    def peer(da, db):
        return (at(da, db), grp)

    def ring(d):
        return (col, plus(z, d, 8) * 2 + core)

    def group(d):
        return (col, plus(grp, d, 16))

    def plane(d):
        return (plus(col, d, 16), grp)

    def go(src, dst, to):
        k = used[0]
        used[0] += 1
        copy = pltpu.make_async_remote_copy(
            src_ref=src, dst_ref=dst, send_sem=send_sem.at[k], recv_sem=recv_sem.at[k],
            device_id=to, device_id_type=MESH,
        )
        copy.start()
        started.append(copy)
        return k

    def landed(k, dst):
        pltpu.make_async_remote_copy(
            src_ref=dst, dst_ref=dst, send_sem=send_sem.at[k], recv_sem=recv_sem.at[k],
            device_id=twin, device_id_type=MESH,
        ).wait_recv()

    loads = [
        pltpu.make_async_copy(src, dst, load_sem.at[i])
        for i, (src, dst) in enumerate(
            (
                (bag_rows.at[:, :, pl.ds(pl.multiple_of(col * 128, 128), 128)], rows_in),
                (bag_mask.at[:, :, pl.ds(pl.multiple_of(col * 128, 128), 128)], mask_in),
                (down_hbm, down),
                (up_hbm, up),
                (top_hbm, top),
            )
        )
    ]
    for load in loads:
        load.start()
    barrier = pltpu.get_barrier_semaphore()
    others = [group(d) for d in range(1, 16)] + [plane(d) for d in range(1, 16)]
    for other in others:
        pl.semaphore_signal(barrier, inc=1, device_id=other, device_id_type=MESH)

    def lanes_of(h, p):
        return pl.ds(pl.multiple_of(h * 4096 + p * 512, 512), 512)

    @pl.loop(0, 16)
    def _(i):
        h, p = lax.div(i, 8), lax.rem(i, 8)
        mine[h, p] = pending[:, lanes_of(h, p)]

    best[...] = jnp.full_like(best, -1)

    @pl.loop(0, 16)
    def _(t):
        dem, slo = upright(demote[pl.ds(t, 1), :]), upright(slot[pl.ds(t, 1), :])
        for j in range(16):
            hit = jnp.where(dem == promote[j : j + 1, :], slo, -1)
            best[j] = jnp.maximum(best[j], jnp.max(hit.reshape(16, 8, 128), axis=0))

    for j in range(16):
        match[j : j + 1, :] = jnp.max(best[j], axis=0, keepdims=True)

    @pl.loop(0, 16)
    def _(t):
        idx = promote[pl.ds(t, 1), :] - grp * 8192
        idx = jnp.where((match[pl.ds(t, 1), :] < 0) & (idx >= 0) & (idx < 8192), idx, -1)
        fetched[t] = pick_lanes(
            idx, 64, lambda s: split(table[:, s * 128 : (s + 1) * 128])
        )

    loads[0].wait()
    loads[1].wait()
    bags[0] = jnp.where(mask_in[...] > 0, rows_in[...], -1)
    pl.semaphore_wait(barrier, len(others))

    k_twin = go(mine.at[1 - core], from_twin, twin)

    k_bags = go(bags.at[0], bags.at[1], twin)

    def stand(which):
        @pl.loop(0, 32)
        def _(i):
            l, f = lax.div(i, 8), lax.rem(i, 8)
            row = upright(bags[which, l, pl.ds(f, 1), :] - core * 4096)
            bag_col[l, pl.ds(pl.multiple_of(which * 1024 + f * 128, 128), 128), :] = row.astype(I16)

    stand(0)
    landed(k_twin, from_twin)
    reduced[...] = mine[core] + from_twin[...]
    k_ring = [go(reduced.at[plus(z, d, 8)], from_ring.at[d], ring(d)) for d in range(1, 8)]

    def count(lo, hi):
        @pl.loop(lo, hi)
        def _(i):
            r = pl.ds(pl.multiple_of(i * 16, 16), 16)
            lane = lax.broadcasted_iota(I32, (16, 128), 1)
            idx = [bag_col[l, r, :].astype(I32) for l in range(4)]
            low = [jnp.where((v & 127) == lane, 1.0, 0.0).astype(BF16) for v in idx]
            high = [(v >> 7).astype(F32).astype(BF16) for v in idx]
            zero = jnp.zeros((16, 128), BF16)
            for t in range(32):
                acc = None
                for l in range(4):
                    hit = jnp.where(high[l] == BF16(t), low[l], zero)
                    acc = hit if acc is None else acc + hit
                counts[r, t * 128 : (t + 1) * 128] = acc

    def origin(ids, first, places, half_rows):
        ids = ids - first
        lane = ids & 127
        high = ids >> 7
        j = lax.broadcasted_iota(I32, (1, 2048), 1)
        sub = lax.broadcasted_iota(I32, (128, 2048), 0)
        here = sub == lane
        major = jnp.where(here, (j >> 7).astype(F32), 0.0).astype(BF16)
        minor = jnp.where(here, (j & 127).astype(F32) + 1.0, 0.0).astype(BF16)
        rows = lax.broadcasted_iota(I32, (half_rows, 2048), 0)
        pick = jnp.where(rows == high, 1.0, 0.0).astype(BF16)
        major = lax.dot_general(pick, major, NT, preferred_element_type=F32)
        minor = lax.dot_general(pick, minor, NT, preferred_element_type=F32)
        return (major * 128.0 + minor).astype(I32) - 1

    def flat(ref):
        return jnp.concatenate([ref[t : t + 1, :] for t in range(16)], axis=1)

    slot_from[...] = origin(flat(slot), core * 4096, 4096, 32)
    home[...] = origin(flat(demote), grp * 8192, 8192, 64)
    count(0, 40)
    total = reduced[z]
    for d in range(1, 8):
        landed(k_ring[d - 1], from_ring.at[d])
        total = total + from_ring[d]
    base = core * 4096 + z * 512
    synced[...] = total + hot[:, pl.ds(pl.multiple_of(base, 512), 512)]

    @pl.loop(0, 16)
    def _(t):
        again = match[pl.ds(t, 1), :] - base
        value = pick_lanes(again, 4, lambda s: split(synced[:, s * 128 : (s + 1) * 128]))
        fetched[t] = value + fetched[t]

    k_fet = [go(fetched.at[plus(grp, d, 16)], fetched_in.at[d], group(d)) for d in range(1, 16)]
    all_synced[grp] = synced[...]
    k_syn = [go(all_synced.at[grp], all_synced.at[grp], ring(d)) for d in range(1, 8)]
    k_hand = [go(all_synced.at[grp], all_synced.at[grp], twin)]
    landed(k_bags, bags.at[1])
    stand(1)
    count(40, 84)
    mine_now = fetched[grp]
    for d in range(1, 16):
        landed(k_fet[d - 1], fetched_in.at[d])
        mine_now = mine_now + fetched_in[d]
    arrived[grp] = mine_now
    k_arr = [go(arrived.at[grp], arrived.at[grp], group(d)) for d in range(1, 16)]
    count(84, 128)
    for d in range(1, 8):
        there = all_synced.at[plus(z, -d, 8) * 2 + core]
        landed(k_syn[d - 1], there)
        k_hand.append(go(there, there, twin))
    for d in range(1, 16):
        landed(k_arr[d - 1], arrived.at[plus(grp, -d, 16)])

    def renew(lo, hi):
        @pl.loop(lo, hi)
        def _(p):
            for i in range(4):
                idx = slot_from[pl.ds(p * 4 + i, 1), :]
                lanes = slice(i * 128, (i + 1) * 128)
                picked = pick_lanes(idx, 16, lambda s: split(arrived[s]))
                old = all_synced[p * 2 + core, :, lanes]
                value = jnp.where(jnp.broadcast_to(idx, (16, 128)) >= 0, picked, old)
                fresh[p, :, lanes] = value
                unit[pl.ds(p * 4 + i, 1), :] = jnp.max(jnp.abs(value), axis=0, keepdims=True)

    def encode():
        units[col] = (jnp.maximum(unit[...], 1e-30) * (1.008 / 32000.0)).astype(BF16)
        unit[...] = 1.0 / units[col].astype(F32)

        @pl.loop(0, 8)
        def _(p):
            for i in range(4):
                lanes = slice(i * 128, (i + 1) * 128)
                code = jnp.round(fresh[p, :, lanes] * unit[pl.ds(p * 4 + i, 1), :])
                full[col, p, :, lanes] = code.astype(I32).astype(I16)

    def decode(c):
        unit_of[...] = units[c].astype(F32)

        @pl.loop(0, 8)
        def _(p):
            for i in range(4):
                lanes = slice(i * 128, (i + 1) * 128)
                value = full[c, p, :, lanes].astype(I32).astype(F32)
                value = value * unit_of[pl.ds(p * 4 + i, 1), :]
                high = value.astype(BF16)
                wide[0, p, c, :, lanes] = high
                wide[1, p, c, :, lanes] = (value - high.astype(F32)).astype(BF16)

    def demoted(lo, hi):
        @pl.loop(lo, hi)
        def _(t):
            evicted[t] = pick_lanes(
                slot[pl.ds(t, 1), :], 64,
                lambda s: split(
                    all_synced[
                        (s % 32 // 4) * 2 + s // 32, :, (s % 4) * 128 : (s % 4 + 1) * 128
                    ]
                ),
            )

    def table_out(lo, hi):
        @pl.loop(lo, hi)
        def _(q):
            for u in range(4):
                lanes = pl.ds(pl.multiple_of(q * 512 + u * 128, 128), 128)
                idx = home[pl.ds(q * 4 + u, 1), :]
                picked = pick_lanes(idx, 16, lambda s: (evicted[s, 0:8, :], evicted[s, 8:16, :]))
                new_table[:, lanes] = jnp.where(
                    jnp.broadcast_to(idx, (16, 128)) >= 0, picked, table[:, lanes]
                )

    def widen():
        half = pl.ds(0, 4), pl.ds(4, 4)

        def block(da, db, which=None):
            ref = full.at[at(da, db)]
            return ref if which is None else ref.at[half[which]]

        def pass_on(ref, to):
            return go(ref, ref, to)

        def along_b(da):
            return pass_on(block(da, 0), peer(0, 1)), pass_on(block(da, 0), peer(0, -1))

        right = pass_on(block(0, 0), peer(1, 0))
        left = pass_on(block(0, 0), peer(-1, 0))
        pairs = {0: along_b(0)}
        more = {}

        def along_b_more(da):
            landed(pairs[da][0], block(da, -1))
            first = pass_on(block(da, -1, 0), peer(0, 1))
            landed(pairs[da][1], block(da, 1))
            more[da] = first, pass_on(block(da, 1, 1), peer(0, -1))
            decode(at(da, -1))
            decode(at(da, 1))

        yield
        decode(col)
        landed(right, block(-1, 0))
        on_right = pass_on(block(-1, 0, 0), peer(1, 0))
        pairs[-1] = along_b(-1)
        yield
        landed(left, block(1, 0))
        on_left = pass_on(block(1, 0, 1), peer(-1, 0))
        pairs[1] = along_b(1)
        yield
        along_b_more(0)
        yield
        landed(on_right, block(2, 0, 0))
        landed(on_left, block(2, 0, 1))
        pairs[2] = along_b(2)
        for da in (-1, 1, 2):
            decode(at(da, 0))
        for da in (-1, 1, 2):
            yield
            along_b_more(da)
        for da in (0, -1, 1, 2):
            yield
            landed(more[da][0], block(da, 2, 0))
            landed(more[da][1], block(da, 2, 1))
            decode(at(da, 2))

    def look(first, out):
        acc = None
        for p in range(8):
            some = counts[pl.ds(pl.multiple_of(first, 512), 512), p * 512 : (p + 1) * 512]
            for k in range(2):
                term = lax.dot_general(
                    some, wide[k, p].reshape(256, 512), NT, preferred_element_type=F32
                )
                acc = term if acc is None else acc + term
        out[...] = acc.reshape(2, 256, 256)

    renew(0, 8)
    encode()
    travel = widen()
    next(travel)
    k_unit = [go(units.at[col], units.at[col], plane(d)) for d in range(1, 16)]
    k_old = go(fresh, old_in, twin)
    for d in range(8):
        landed(k_hand[d], all_synced.at[plus(z, -d, 8) * 2 + 1 - core])
    next(travel)
    next(travel)
    for d in range(1, 16):
        landed(k_unit[d - 1], units.at[plus(col, -d, 16)])
    for _ in travel:
        pass

    k_pool = []

    @pl.loop(0, 2)
    def _(m):
        look(1024 + m * 512, for_twin.at[pl.ds(m * 2, 2)])

    for m in range(4):
        k_pool.append(go(for_twin.at[m], pooled_in.at[m], twin))

    @pl.loop(0, 2)
    def _(m):
        look(m * 512, pooled.at[pl.ds(m * 2, 2)])

    for m in range(4):
        landed(k_pool[m], pooled_in.at[m])

    for load in loads[2:]:
        load.wait()
    both = [(pooled[m] + pooled_in[m]).astype(BF16) for m in range(4)]
    x0_ref[...] = jnp.concatenate(
        [both[f // 2][f % 2 * 128 : f % 2 * 128 + 128] for f in range(8)], axis=1
    )
    low = jnp.dot(x0_ref[...], down[...], preferred_element_type=F32).astype(BF16)

    def lanes_at(i, size):
        return pl.ds(pl.multiple_of(i * size, size), size)

    @pl.loop(0, 4)
    def _(i):
        lanes = lanes_at(i, 512)
        gate = jnp.dot(low, up[:, lanes], preferred_element_type=F32) + cross_bias[:, lanes]
        gate_ref[:, lanes] = gate
        wide0 = x0_ref[:, lanes].astype(F32)
        x1_ref[:, lanes] = (wide0 * gate + wide0).astype(BF16)

    @pl.loop(0, 4)
    def _(i):
        lanes = lanes_at(i, 256)
        pre_ref[:, lanes] = (
            jnp.dot(x1_ref[...], top[:, lanes], preferred_element_type=F32) + top_bias[:, lanes]
        )

    pre = pre_ref[...]
    sig = jax.nn.sigmoid(pre)
    hidden = (pre * sig).astype(BF16).astype(F32)
    weight = out_weight[...].astype(F32).reshape(1, 1024)
    logit = jnp.sum(hidden * weight, axis=1, keepdims=True)
    across = jnp.broadcast_to(logit, (128, 128)).T
    logits[...] = across[0:1, :]
    dlogit = jax.nn.sigmoid(across) - label[...].astype(F32)
    dlogit = dlogit.T[:, 0:1]
    slope = sig * (1.0 + pre * (1.0 - sig))
    dhidden = (dlogit * weight * slope).astype(BF16)

    @pl.loop(0, 4)
    def _(i):
        lanes = lanes_at(i, 512)
        dx1 = lax.dot_general(dhidden, top[lanes, :], NT, preferred_element_type=F32)
        dx1_ref[:, lanes] = dx1
        x1_ref[:, lanes] = (dx1 * x0_ref[:, lanes].astype(F32)).astype(BF16)

    dlow = lax.dot_general(x1_ref[...], up[...], NT, preferred_element_type=F32).astype(BF16)
    k_back = []
    for c in range(4):
        lanes = slice(c * 512, (c + 1) * 512)
        dx0 = dx1_ref[:, lanes] * (gate_ref[:, lanes] + 1.0) + lax.dot_general(
            dlow, down[lanes, :], NT, preferred_element_type=F32
        )
        for f in range(2):
            back[c, :, f * 128 : (f + 1) * 128] = dx0[:, f * 256 : (f + 1) * 256].T.astype(BF16)
        k_back.append(go(back.at[c], back.at[4 + c], twin))

    for c in range(4):
        landed(k_back[c], back.at[4 + c])

    def slopes(lo, hi):
        @pl.loop(lo, hi)
        def _(p):
            lanes = pl.ds(pl.multiple_of(p * 512, 512), 512)
            acc = None
            for c in range(8):
                term = jnp.dot(
                    back[c], counts[c * 256 : (c + 1) * 256, lanes], preferred_element_type=F32
                )
                acc = term if acc is None else acc + term
            grads[:, p] = acc.astype(BF16).reshape(16, 16, 512)

    def add(ref, other):
        ref[...] = (ref[...].astype(F32) + other[...].astype(F32)).astype(BF16)

    order = [(da, db) for da in (2, 1, -1, 0) for db in (2, 1, -1, 0)]

    def narrow(s):
        whole = pl.ds(s * N, N)
        lo, hi = pl.ds(s * N, N // 2), pl.ds(s * N + N // 2, N // 2)
        few = pl.ds(s * N // 2, N // 2)
        ways = [{} for _ in range(4)]
        last = {}

        def first_part(i):
            for j in range(4):
                k = i * 4 + j
                where = at(*order[k])
                if j == 0:
                    ways[i][0] = go(grads.at[where, lo], fwd_in.at[i, 0, few], peer(0, 1))
                    ways[i][1] = go(grads.at[where, hi], fwd_in.at[i, 1, few], peer(0, -1))
                if j == 1:
                    ways[i][2] = go(grads.at[where, hi], side_in.at[i, 0, hi], peer(0, 1))
                if j == 2:
                    ways[i][3] = go(grads.at[where, lo], side_in.at[i, 1, lo], peer(0, -1))

        def second_part(i):
            landed(ways[i][0], fwd_in.at[i, 0, few])
            add(grads.at[at(*order[i * 4 + 1]), lo], fwd_in.at[i, 0, few])
            ways[i][4] = go(grads.at[at(*order[i * 4 + 1]), lo], side_in.at[i, 0, lo], peer(0, 1))
            landed(ways[i][1], fwd_in.at[i, 1, few])
            add(grads.at[at(*order[i * 4 + 2]), hi], fwd_in.at[i, 1, few])
            ways[i][5] = go(grads.at[at(*order[i * 4 + 2]), hi], side_in.at[i, 1, hi], peer(0, -1))

        def third_part(i):
            landed(ways[i][2], side_in.at[i, 0, hi])
            landed(ways[i][3], side_in.at[i, 1, lo])
            landed(ways[i][4], side_in.at[i, 0, lo])
            landed(ways[i][5], side_in.at[i, 1, hi])
            where = at(*order[i * 4 + 3])
            grads[where, whole] = (
                grads[where, whole].astype(F32)
                + side_in[i, 0, whole].astype(F32)
                + side_in[i, 1, whole].astype(F32)
            ).astype(BF16)

        def last_axis(i):
            where = at(*order[i * 4 + 3])
            if i == 0:
                last[0] = go(grads.at[where, lo], far_in.at[0, few], peer(1, 0))
                last[1] = go(grads.at[where, hi], far_in.at[1, few], peer(-1, 0))
            if i == 1:
                last[2] = go(grads.at[where, hi], lane_in.at[0, hi], peer(1, 0))
                landed(last[0], far_in.at[0, few])
                add(grads.at[where, lo], far_in.at[0, few])
                last[4] = go(grads.at[where, lo], lane_in.at[0, lo], peer(1, 0))
            if i == 2:
                last[3] = go(grads.at[where, lo], lane_in.at[1, lo], peer(-1, 0))
                landed(last[1], far_in.at[1, few])
                add(grads.at[where, hi], far_in.at[1, few])
                last[5] = go(grads.at[where, hi], lane_in.at[1, hi], peer(-1, 0))

        def begin():
            for i in range(4):
                first_part(i)

        def more(*parts):
            for i in parts:
                second_part(i)

        def turn(i):
            third_part(i)
            last_axis(i)

        def finish():
            turn(3)
            landed(last[2], lane_in.at[0, hi])
            landed(last[3], lane_in.at[1, lo])
            landed(last[4], lane_in.at[0, lo])
            landed(last[5], lane_in.at[1, hi])
            ring_out[whole] = (
                grads[col, whole].astype(F32)
                + lane_in[0, whole].astype(F32)
                + lane_in[1, whole].astype(F32)
            ).astype(BF16)

        return begin, more, turn, finish

    slopes(0, 4)
    begin0, more0, turn0, finish0 = narrow(0)
    begin1, more1, turn1, finish1 = narrow(1)
    begin0()
    slopes(4, 6)
    more0(0, 1)
    slopes(6, 8)
    begin1()
    more0(2, 3)
    turn0(0)
    turn0(1)
    more1(0, 1)
    turn0(2)
    more1(2, 3)
    turn1(0)
    turn1(1)
    finish0()
    turn1(2)
    finish1()

    k_ring = [go(ring_out.at[plus(z, d, 8)], ring_in.at[d], ring(d)) for d in range(1, 8)]
    demoted(0, 16)
    grad = ring_out[z].astype(F32)
    for d in range(1, 8):
        landed(k_ring[d - 1], ring_in.at[d])
        grad = grad + ring_in[d].astype(F32)
    square = jnp.sum(grad * grad, axis=0, keepdims=True)
    square = [square[:, i * 128 : (i + 1) * 128] for i in range(4)]
    squares[col] = jnp.concatenate(square + square, axis=0)
    k_sq = [go(squares.at[col], squares.at[col], plane(d)) for d in range(1, 16)]
    all_grads[grp] = grad.astype(BF16)
    k_all = [go(all_grads.at[grp], all_grads.at[grp], ring(d)) for d in range(1, 8)]
    k_hand = [go(all_grads.at[grp], all_grads.at[grp], twin)]
    table_out(0, 9)
    for d in range(1, 16):
        landed(k_sq[d - 1], squares.at[plus(col, -d, 16)])
    before = accum[pl.ds(core * 32 + z * 4, 4), :]
    sums[grp] = jnp.concatenate([before, before], axis=0) + jnp.sum(squares[...], axis=0) / E
    k_sum = [go(sums.at[grp], sums.at[grp], group(d)) for d in range(1, 16)]
    table_out(9, 16)
    for d in range(1, 8):
        there = all_grads.at[plus(z, -d, 8) * 2 + core]
        landed(k_all[d - 1], there)
        k_hand.append(go(there, there, twin))
    for d in range(8):
        landed(k_hand[d], all_grads.at[plus(z, -d, 8) * 2 + 1 - core])
    for d in range(1, 16):
        landed(k_sum[d - 1], sums.at[plus(grp, -d, 16)])
    landed(k_old, old_in)
    for h in range(2):
        for p in range(8):
            new_accum[h * 32 + p * 4 : h * 32 + p * 4 + 4, :] = sums[p * 2 + h, 0:4, :]

        @pl.loop(0, 8)
        def _(p):
            g = p * 2 + h
            for i in range(4):
                lanes = pl.ds(pl.multiple_of(h * 4096 + p * 512 + i * 128, 128), 128)
                inner = slice(i * 128, (i + 1) * 128)
                scale = STEP / jnp.sqrt(sums[g, i : i + 1, :] + EPS)
                old = jnp.where(core == h, fresh[p, :, inner], old_in[p, :, inner])
                new_hot[:, lanes] = old - all_grads[g, :, inner].astype(F32) * scale

    for copy in started:
        copy.wait_send()


def step(*args):
    dma = pltpu.SemaphoreType.DMA
    v = pltpu.VMEM
    return pl.pallas_call(
        step_kernel,
        out_shape=[
            jax.ShapeDtypeStruct((16, 8192), F32),
            jax.ShapeDtypeStruct((16, 8192), F32),
            jax.ShapeDtypeStruct((64, 128), F32),
            jax.ShapeDtypeStruct((1, 128), F32),
        ],
        in_specs=[VMEM] * 11 + [ANY] * 5,
        out_specs=[VMEM] * 4,
        scratch_shapes=[
            v((2048, 512), BF16),
            v((512, 2048), BF16),
            v((2048, 1024), BF16),
            v((4, 8, 128), I32),
            v((4, 8, 128), I32),
            v((2, 8, 16, 512), F32),
            v((8, 16, 512), F32),
            v((8, 16, 512), F32),
            v((8, 16, 512), F32),
            v((16, 512), F32),
            v((16, 16, 128), F32),
            v((16, 16, 128), F32),
            v((16, 16, 128), F32),
            v((16, 128), I32),
            v((16, 8, 128), I32),
            v((32, 128), I32),
            v((2, 4, 8, 128), I32),
            v((16, 16, 512), F32),
            v((16, 8, 16, 512), I16),
            v((8, 16, 512), F32),
            v((8, 16, 512), F32),
            v((32, 128), F32),
            v((16, 32, 128), BF16),
            v((32, 128), F32),
            v((2, 8, 16, 16, 512), BF16),
            v((4, 2048, 128), I16),
            v((2048, 4096), BF16),
            v((4, 256, 256), F32),
            v((4, 256, 256), F32),
            v((4, 256, 256), F32),
            v((8, 256, 256), BF16),
            v((16, 8, 16, 512), BF16),
            v((128, 2048), BF16),
            v((128, 2048), BF16),
            v((128, 2048), F32),
            v((128, 2048), F32),
            v((128, 1024), F32),
            v((16, 16, 128), F32),
            v((64, 128), I32),
            v((4, 2, 4, 16, 512), BF16),
            v((4, 2, 8, 16, 512), BF16),
            v((2, 8, 16, 512), BF16),
            v((2, 4, 16, 512), BF16),
            v((8, 16, 512), BF16),
            v((8, 16, 512), BF16),
            v((16, 16, 512), BF16),
            v((16, 8, 128), F32),
            v((16, 8, 128), F32),
            dma((5,)),
            dma((N_SEM,)),
            dma((N_SEM,)),
        ],
        compiler_params=pltpu.CompilerParams(
            collective_id=0, has_side_effects=True, vmem_limit_bytes=62 << 20
        ),
    )(*args)


def hand_out_kernel(*refs):
    n = len(refs) // 2
    for i in range(n):
        refs[n + i][...] = refs[i][...]


def hand_out(*arrays):
    return pl.pallas_call(
        hand_out_kernel,
        out_shape=[jax.ShapeDtypeStruct(a.shape, a.dtype) for a in arrays],
        in_specs=[VMEM] * len(arrays),
        out_specs=[VMEM] * len(arrays),
    )(*arrays)


def per_device(
    table, hot, accum, pending, slot_ids, demote_ids, promote_ids, bag_rows, bag_mask, labels,
    cross_down, cross_up, cross_bias, top_weight, top_bias, out_weight,
):
    outputs = step(
        pending[0], table, hot, accum.reshape(64, 128), slot_ids.reshape(16, 128),
        demote_ids.reshape(16, 128), promote_ids.reshape(16, 128), labels, cross_bias[None],
        top_bias[None], out_weight, bag_rows, bag_mask, cross_down, cross_up, top_weight,
    )
    new_table, new_hot, new_accum, logits = hand_out(*outputs)
    return new_table, new_hot, new_accum.reshape(8192), logits


def solution(mesh):
    return jax.shard_map(
        per_device,
        mesh=mesh,
        in_specs=(
            P("col", "grp"), P("col", None), P(), P("grp", "col", None), P(), P(), P(),
            P(None, None, "grp"), P(None, None, "grp"), P("col", "grp"),
            P(), P(), P(), P(), P(), P(),
        ),
        out_specs=(P("col", "grp"), P("col", None), P(), P("col", "grp")),
        check_vma=False,
    )
```
